32 devices in a mesh: gx: 2 (over x), gy: 4 (over y, core), gz: 4 (over z).
Axes of the slice: x: 2, y: 2, z: 4, core: 2. Of those that a mesh axis runs over, the one named last changes fastest.
Arguments:
- body_local: float32 [3, 4, 8, 16, 128], P(None, 'gx', 'gy', 'gz'), as said below
- charges: float32 [4, 8, 16, 128], P('gx', 'gy', 'gz'), may hold values from -1 to 1
- radii: float32 [4, 8, 16, 128], P('gx', 'gy', 'gz'), may hold values from 0.05 to 0.15
- body_slot: int32 [4, 8, 16, 128], P('gx', 'gy', 'gz'), may hold values from 0 to 647, as said below
- cell_counts: int32 [4, 8, 16], P('gx', 'gy', 'gz'), may hold values from 16 to 128, as said below
- poses: float32 [12, 768], P(None, ('gx', 'gy', 'gz')), as said below
- mobility: float32 [2, 768], P(None, ('gx', 'gy', 'gz')), may hold values from 0.5 to 2
- noise: float32 [6, 768], P(None, ('gx', 'gy', 'gz')), may hold values from -1 to 1
Outputs:
- stepped_poses: float32 [12, 768], P(None, ('gx', 'gy', 'gz'))
- positions: float32 [3, 4, 8, 16, 128], P(None, 'gx', 'gy', 'gz')
The draws below stay inside these ranges and needn't reach their ends.
Inputs may be any that keep to these rules, and one draw needn't show every extreme that they name: Every atom slot belongs to a body owned by its own device or by one of the devices next to it along each axis, periodically; body_slot = (9 (dx + 1) + 3 (dy + 1) + (dz + 1)) * 24 + k names body k of the device at offset (dx, dy, dz). `cell_counts`: slots 0 to count - 1 of a cell hold atoms; the other slots are empty. `poses`: rows 0 to 8 form a rotation matrix; the centre lies inside the brick of the owner device. `body_local`: R local + t of every slot lies, up to whole periods of the box, inside the slot's cell.
All inputs are finite; a program needn't handle non-finite values.
Results may differ from the reference program's by a relative error of at most 0.0003.
Values sent between devices are 32-bit elements; how exact they have to be, the bound alone decides.
No kernel may reach another device: no remote copies, remote signals or barrier semaphores. Data moves between devices by JAX's collectives and lax.ppermute only.
A program may use at most 64 MiB of HBM per device.

```python
import math
import jax
import jax.numpy as jnp
from jax import lax

BRICK_CELLS_X = 2
CY = 2
CZ = 4
NB_DEV = 24
ATOMS_PER_CELL = 128
BOX_CELLS_X = 4
BOX_CELLS_Y = 8
BOX_CELLS_Z = 16
NBODY = 768
N_GX = 2
N_GY = 4
N_GZ = 4


def body_poses(key):
    quat = jax.random.normal(jax.random.fold_in(key, 11), (4, NBODY), jnp.float32)
    quat = quat / jnp.sqrt(jnp.sum(quat * quat, axis=0))
    qw, qx, qy, qz = (quat[0], quat[1], quat[2], quat[3])
    rotation = jnp.stack([1 - 2 * (qy * qy + qz * qz), 2 * (qx * qy - qz * qw), 2 * (qx * qz + qy * qw), 2 * (qx * qy + qz * qw), 1 - 2 * (qx * qx + qz * qz), 2 * (qy * qz - qx * qw), 2 * (qx * qz - qy * qw), 2 * (qy * qz + qx * qw), 1 - 2 * (qx * qx + qy * qy)])
    count_y = BOX_CELLS_Y // CY
    count_z = BOX_CELLS_Z // CZ
    device = jnp.arange(NBODY, dtype=jnp.int32) // NB_DEV
    brick_x = device // (count_y * count_z)
    brick_y = device // count_z % count_y
    brick_z = device % count_z
    target_slot = jax.random.uniform(jax.random.fold_in(key, 12), (3, NBODY), jnp.float32)
    centre = jnp.stack([(brick_x + target_slot[0]) * BRICK_CELLS_X, (brick_y + target_slot[1]) * CY, (brick_z + target_slot[2]) * CZ])
    return jnp.concatenate([rotation, centre], axis=0).astype(jnp.float32)


def atom_slots(key):
    array_shape = (BOX_CELLS_X, BOX_CELLS_Y, BOX_CELLS_Z, ATOMS_PER_CELL)
    at_home = jax.random.randint(jax.random.fold_in(key, 21), array_shape, 0, 2)
    code = jnp.where(at_home == 1, 13, jax.random.randint(jax.random.fold_in(key, 22), array_shape, 0, 27))
    member = jax.random.randint(jax.random.fold_in(key, 23), array_shape, 0, NB_DEV)
    return (code * NB_DEV + member).astype(jnp.int32)


def draw_poses(key, part):
    return body_poses(key)


def draw_body_slot(key, part):
    return atom_slots(key)


def draw_cell_counts(key, part):
    slot_counts = jax.random.randint(jax.random.fold_in(key, 31), (BOX_CELLS_X, BOX_CELLS_Y, BOX_CELLS_Z), 16, ATOMS_PER_CELL + 1)
    cell_index_x = jnp.arange(BOX_CELLS_X)[:, None, None] % BRICK_CELLS_X == 0
    cell_y = jnp.arange(BOX_CELLS_Y)[None, :, None] % CY == 0
    cell_z = jnp.arange(BOX_CELLS_Z)[None, None, :] % CZ == 0
    return jnp.where(cell_index_x & cell_y & cell_z, ATOMS_PER_CELL, slot_counts).astype(jnp.int32)


def draw_body_local(key, part):
    pose_rows = body_poses(key)
    slots = atom_slots(key)
    count_along_x = BOX_CELLS_X // BRICK_CELLS_X
    count_y = BOX_CELLS_Y // CY
    count_z = BOX_CELLS_Z // CZ
    cell_index_x = jnp.arange(BOX_CELLS_X, dtype=jnp.int32)[:, None, None, None]
    cell_y = jnp.arange(BOX_CELLS_Y, dtype=jnp.int32)[None, :, None, None]
    cell_z = jnp.arange(BOX_CELLS_Z, dtype=jnp.int32)[None, None, :, None]
    code = slots // NB_DEV
    member = slots % NB_DEV
    owner_x = (cell_index_x // BRICK_CELLS_X + code // 9 - 1) % count_along_x
    owner_y = (cell_y // CY + code // 3 % 3 - 1) % count_y
    owner_z = (cell_z // CZ + code % 3 - 1) % count_z
    body_ids = (((owner_x * count_y + owner_y) * count_z + owner_z) * NB_DEV + member).reshape(-1)
    target_slot = jax.random.uniform(jax.random.fold_in(key, 41), (3, BOX_CELLS_X, BOX_CELLS_Y, BOX_CELLS_Z, ATOMS_PER_CELL), jnp.float32)
    zero_buffer = jnp.zeros((BOX_CELLS_X, BOX_CELLS_Y, BOX_CELLS_Z, ATOMS_PER_CELL), jnp.float32)
    target = jnp.stack([cell_index_x + zero_buffer, cell_y + zero_buffer, cell_z + zero_buffer]) + target_slot
    chosen = jnp.take(pose_rows, body_ids, axis=1)
    delta = target.reshape(3, -1) - chosen[9:12]
    domain_extent = jnp.array([BOX_CELLS_X, BOX_CELLS_Y, BOX_CELLS_Z], jnp.float32)[:, None]
    delta = delta - domain_extent * jnp.floor(delta / domain_extent + 0.5)
    resident_rows = jnp.stack([chosen[col_at] * delta[0] + chosen[3 + col_at] * delta[1] + chosen[6 + col_at] * delta[2] for col_at in range(3)])
    return resident_rows.reshape(3, BOX_CELLS_X, BOX_CELLS_Y, BOX_CELLS_Z, ATOMS_PER_CELL).astype(jnp.float32)


def block_scale(rng, shape, cuts, smallest, largest):
    level, own = 1.0, jax.random.fold_in(rng, 6)
    for position, blocks in cuts:
        heights = jnp.exp(jax.random.uniform(jax.random.fold_in(own, position), (blocks,), jnp.float32, smallest / len(cuts), largest / len(cuts)))
        level = level * jnp.repeat(heights, shape[position] // blocks).reshape([-1 if axis == position else 1 for axis in range(len(shape))])
    return level


def normal_values(stream_key, extent, spread, limit, split=(), held_as=jnp.bfloat16):
    values = spread * jax.random.normal(stream_key, extent, jnp.float32)
    if split:
        values = values * block_scale(stream_key, extent, split, -0.22, 0.18)
    return jnp.clip(values, -limit, limit).astype(held_as)


def setup_inputs(seed: int = 0) -> dict:
    arg_keys = jax.random.split(jax.random.key(seed), 9)
    body_local = draw_body_local(jax.random.fold_in(arg_keys[8], 71), 0)
    charges = jnp.clip(jax.random.uniform(arg_keys[1], (BOX_CELLS_X, BOX_CELLS_Y, BOX_CELLS_Z, ATOMS_PER_CELL), jnp.float32, -1.0, 1.0) * block_scale(arg_keys[1], (BOX_CELLS_X, BOX_CELLS_Y, BOX_CELLS_Z, ATOMS_PER_CELL), ((0, 2), (1, 4), (2, 4)), -0.4, 0.0), -1.0, 1.0)
    radii = jnp.clip(jnp.exp(math.log(0.15) - 1.0986123 * jax.random.uniform(arg_keys[2], (BOX_CELLS_X, BOX_CELLS_Y, BOX_CELLS_Z, ATOMS_PER_CELL), jnp.float32) ** block_scale(arg_keys[2], (BOX_CELLS_X, BOX_CELLS_Y, BOX_CELLS_Z, ATOMS_PER_CELL), ((0, 2), (1, 4), (2, 4)), -0.2, 0.2)), 0.05, 0.15)
    body_slot = draw_body_slot(jax.random.fold_in(arg_keys[8], 71), 0)
    cell_counts = draw_cell_counts(jax.random.fold_in(arg_keys[8], 71), 0)
    poses = draw_poses(jax.random.fold_in(arg_keys[8], 71), 0)
    mobility = jnp.clip(jnp.exp(math.log(2.0) - 1.3862944 * jax.random.uniform(arg_keys[6], (2, NBODY), jnp.float32) ** block_scale(arg_keys[6], (2, NBODY), ((1, 32),), -0.2, 0.2)), 0.5, 2.0)
    noise = normal_values(arg_keys[7], (6, NBODY), 0.2, 1.0, ((1, 32),), jnp.float32)
    return dict(body_local=body_local, charges=charges, radii=radii, body_slot=body_slot, cell_counts=cell_counts, poses=poses, mobility=mobility, noise=noise)


min_reach = 0.15
clash_gain = 20.0
debye_length = 0.5
move_gain = 0.02
turn_gain = 0.01

def pair_force(own_cells, other_cells, domain_extent):
    delta = own_cells[0:3, :, :, None] - other_cells[0:3, :, None, :]
    delta = delta - domain_extent * jnp.floor(delta / domain_extent + 0.5)
    dist_sq = lax.optimization_barrier(jnp.sum(delta * delta, axis=0))
    dist = jnp.sqrt(dist_sq)
    reach = jnp.maximum(dist, min_reach)
    switch = jnp.square(jnp.maximum(1.0 - dist_sq, 0.0))
    sigma = own_cells[4][:, :, None] + other_cells[4][:, None, :]
    clash = clash_gain * jnp.maximum(sigma - dist, 0.0)
    screened = own_cells[3][:, :, None] * other_cells[3][:, None, :] * jnp.exp(-dist / debye_length) * (1.0 / reach + 1.0 / debye_length) / reach * switch
    weight = own_cells[5][:, :, None] * other_cells[5][:, None, :] * (clash + screened) / reach
    return lax.optimization_barrier(jnp.sum(weight[None] * delta, axis=-1))

def place_atoms(pose_rows, resident_rows):
    arm_rows = jnp.stack([pose_rows[3 * row_at] * resident_rows[0] + pose_rows[3 * row_at + 1] * resident_rows[1] + pose_rows[3 * row_at + 2] * resident_rows[2] for row_at in range(3)])
    return (arm_rows, arm_rows + pose_rows[9:12])

def cross_rows(first_rows, second_rows):
    return jnp.stack([first_rows[1] * second_rows[2] - first_rows[2] * second_rows[1], first_rows[2] * second_rows[0] - first_rows[0] * second_rows[2], first_rows[0] * second_rows[1] - first_rows[1] * second_rows[0]])

def advance(pose_rows, totals, mobility, noise):
    centre = pose_rows[9:12] + move_gain * mobility[0] * totals[0:3] + noise[0:3]
    spin = 0.5 * (turn_gain * mobility[1] * totals[3:6] + noise[3:6])
    spin_sq = lax.optimization_barrier(jnp.sum(spin * spin, axis=0))
    factor = 2.0 / (1.0 + spin_sq)
    skew_mat = [[None, -spin[2], spin[1]], [spin[2], None, -spin[0]], [-spin[1], spin[0], None]]
    turn = []
    for row_at in range(3):
        line = []
        for col_at in range(3):
            inner = spin[row_at] * spin[col_at]
            if row_at == col_at:
                line.append(1.0 + factor * (inner - spin_sq))
            else:
                line.append(factor * (skew_mat[row_at][col_at] + inner))
        turn.append(line)
    rotated = []
    for row_at in range(3):
        for col_at in range(3):
            rotated.append(turn[row_at][0] * pose_rows[col_at] + turn[row_at][1] * pose_rows[3 + col_at] + turn[row_at][2] * pose_rows[6 + col_at])
    return jnp.concatenate([jnp.stack(rotated), centre], axis=0)

def owner_ids(body_slot):
    cell_index_x = jnp.arange(BOX_CELLS_X, dtype=jnp.int32)[:, None, None, None]
    cell_y = jnp.arange(BOX_CELLS_Y, dtype=jnp.int32)[None, :, None, None]
    cell_z = jnp.arange(BOX_CELLS_Z, dtype=jnp.int32)[None, None, :, None]
    code = body_slot // NB_DEV
    member = body_slot % NB_DEV
    owner_x = (cell_index_x // BRICK_CELLS_X + code // 9 - 1) % N_GX
    owner_y = (cell_y // CY + code // 3 % 3 - 1) % N_GY
    owner_z = (cell_z // CZ + code % 3 - 1) % N_GZ
    return (((owner_x * N_GY + owner_y) * N_GZ + owner_z) * NB_DEV + member).astype(jnp.int32)

def reference(body_local, charges, radii, body_slot, cell_counts, poses, mobility, noise):
    body_ids = owner_ids(body_slot).reshape(-1)
    resident_rows = body_local.reshape(3, -1)
    arm_rows, placement_index = place_atoms(jnp.take(poses, body_ids, axis=1), resident_rows)
    slot_iota = jnp.arange(ATOMS_PER_CELL, dtype=jnp.int32)[None, None, None, :]
    filled_slots = (slot_iota < cell_counts[..., None]).astype(charges.dtype)
    message_rows = jnp.concatenate([placement_index.reshape(3, BOX_CELLS_X, BOX_CELLS_Y, BOX_CELLS_Z, ATOMS_PER_CELL), charges[None], radii[None], filled_slots[None]], axis=0)
    domain_extent = jnp.array([BOX_CELLS_X, BOX_CELLS_Y, BOX_CELLS_Z], dtype=message_rows.dtype)[:, None, None, None]
    flattened_owned = jnp.moveaxis(message_rows, 1, 0).reshape(BOX_CELLS_X, 6, BOX_CELLS_Y * BOX_CELLS_Z, ATOMS_PER_CELL)

    def visit(running, offset_code):
        step_x = offset_code // 9 - 1
        step_y = offset_code // 3 % 3 - 1
        step_z = offset_code % 3 - 1
        neighbour_block = jnp.roll(message_rows, (-step_x, -step_y, -step_z), axis=(1, 2, 3))
        flattened_neighbour = jnp.moveaxis(neighbour_block, 1, 0).reshape(BOX_CELLS_X, 6, BOX_CELLS_Y * BOX_CELLS_Z, ATOMS_PER_CELL)
        part_force = lax.map(lambda pair: pair_force(pair[0], pair[1], domain_extent), (flattened_owned, flattened_neighbour))
        return (running + part_force, None)
    start_offset = jnp.zeros((BOX_CELLS_X, 3, BOX_CELLS_Y * BOX_CELLS_Z, ATOMS_PER_CELL), message_rows.dtype)
    force_rows = lax.scan(visit, start_offset, jnp.arange(27, dtype=jnp.int32))[0]
    force = jnp.moveaxis(force_rows, 1, 0).reshape(3, -1)
    torque = cross_rows(arm_rows, force)
    contrib = jnp.concatenate([force, torque], axis=0)
    totals = jax.ops.segment_sum(contrib.T, body_ids, num_segments=NBODY).T
    stepped_poses = advance(poses, totals, mobility, noise)
    moved_arm, shifted_poses = place_atoms(jnp.take(stepped_poses, body_ids, axis=1), resident_rows)
    return (stepped_poses, shifted_poses.reshape(3, BOX_CELLS_X, BOX_CELLS_Y, BOX_CELLS_Z, ATOMS_PER_CELL))
```

```python
import functools
import math

import jax
import jax.numpy as jnp
from jax import lax
from jax.experimental import pallas as pl
from jax.experimental.pallas import tpu as pltpu
from jax.sharding import PartitionSpec as P

min_reach = 0.15
clash_gain = 20.0
debye_length = 0.5
move_gain = 0.02
turn_gain = 0.01

LANES = 128
ROWS = 8
POSE_ROWS = 24
SEGMENT = 32
SCALE = 1.0 / (debye_length * math.log(2.0))
CHARGE_SCALE = math.sqrt(1.0 / (clash_gain * SCALE))
EMPTY = -20.0

f32 = jnp.float32
i32 = jnp.int32


def window(count):
    return min(count, 4)


def prep_kernel(sizes, coords, counts, local, charges, radii, slots, poses, mobility, noise, own, message):
    cells_x, cells_y, cells_z, owned = sizes
    lane = lax.broadcasted_iota(i32, (cells_z, LANES), 1)
    row = lax.broadcasted_iota(i32, (cells_z, LANES), 0)
    for x in range(cells_x):
        for y in range(cells_y):
            base = (x * cells_y + y) * cells_z * ROWS
            held = jnp.zeros((cells_z, LANES), i32)
            for z in range(cells_z):
                held = jnp.where(row == z, counts[(x * cells_y + y) * cells_z + z], held)
            filled = lane < held
            slot = slots[x, y].astype(f32)
            offset = jnp.floor((slot + 0.5) * (1.0 / owned))
            body = slot - offset * owned
            step_x = jnp.floor((offset + 0.5) * (1.0 / 9.0))
            step_y = jnp.floor((offset - 9.0 * step_x + 0.5) * (1.0 / 3.0))
            step_z = offset - 9.0 * step_x - 3.0 * step_y
            code = body + 32.0 * step_z + 128.0 * step_y + 512.0 * step_x
            rows = [
                local[0, x, y],
                local[1, x, y],
                local[2, x, y],
                jnp.where(filled, charges[x, y], 0.0),
                jnp.where(filled, radii[x, y], EMPTY / SCALE),
                code,
                held.astype(f32),
                jnp.zeros((cells_z, LANES), f32),
            ]
            for k, value in enumerate(rows):
                own[pl.ds(base + k, cells_z, stride=ROWS), :] = value
            face = (x * cells_y + y) * ROWS
            message[face : face + ROWS, :] = own[base : base + ROWS, :]
    at = cells_x * cells_y * ROWS
    message[at:, :] = jnp.zeros((POSE_ROWS, LANES), f32)
    message[at : at + 12, :owned] = poses[...]
    message[at + 12 : at + 14, :owned] = mobility[...]
    message[at + 14 : at + 20, :owned] = noise[...]
    message[at:, :] = pltpu.roll(message[at:, :], coords[2] * SEGMENT, axis=1)


def lookup(table_row, lane_at, chunk_at, chunks):
    value = None
    for chunk in range(chunks):
        row = jnp.broadcast_to(table_row(chunk), lane_at.shape)
        picked = jnp.take_along_axis(row, lane_at, axis=1)
        value = picked if value is None else jnp.where(chunk_at == chunk, picked, value)
    return value


def pair_terms(column, row, dist_floor):
    dx = column[0] - row[0]
    dy = column[1] - row[1]
    dz = column[2] - row[2]
    dist_sq = dx * dx + dy * dy + dz * dz
    inverse = lax.rsqrt(jnp.maximum(dist_sq, 1e-30))
    dist = dist_sq * inverse
    inv_reach = jnp.minimum(inverse, 1.0 / dist_floor)
    gap = (column[3] + row[3]) - dist
    cut = jnp.maximum(SCALE * SCALE - dist_sq, 0.0)
    screened = (column[4] * row[4]) * jnp.exp2(gap) * (cut * cut)
    weight = inv_reach * (jnp.maximum(gap, 0.0) + screened * ((inv_reach + math.log(2.0)) * inv_reach))
    return weight * dx, weight * dy, weight * dz


def pair_kernel(
    sizes, coords, own, halo_z, halo_y, halo_x, table, out,
    raw, pos, arms, lane_at, chunk_at, held, columns, row_force, column_force, moved, contrib,
):
    cells_x, cells_y, cells_z, count_x, count_y, count_z = sizes
    wide_x, wide_y, wide_z = window(count_x), window(count_y), window(count_z)
    chunks = wide_x * wide_y
    ext_y, ext_z = cells_y + 1, cells_z + 1
    cells = (cells_x + 1) * ext_y * ext_z
    padded = raw.shape[0] // ROWS

    def at(x, y, z):
        return (x * ext_y + y) * ext_z + z

    def put(cell, ref, index):
        raw[cell * ROWS : (cell + 1) * ROWS, :] = ref[index * ROWS : (index + 1) * ROWS, :]

    for x in range(cells_x + 1):
        for y in range(ext_y):
            for z in range(ext_z):
                if x == cells_x:
                    put(at(x, y, z), halo_x, y * ext_z + z)
                elif y == cells_y:
                    put(at(x, y, z), halo_y, x * ext_z + z)
                elif z == cells_z:
                    put(at(x, y, z), halo_z, x * cells_y + y)
                else:
                    put(at(x, y, z), own, (x * cells_y + y) * cells_z + z)
    for cell in range(cells, padded):
        raw[cell * ROWS : (cell + 1) * ROWS, :] = jnp.zeros((ROWS, LANES), f32)
    for cell in range(cells):
        held[cell] = jnp.max(raw[cell * ROWS + 6 : cell * ROWS + 7, :]).astype(i32)

    coord_x, coord_y, coord_z = coords[0], coords[1], coords[2]

    def place(group, carry):
        first = pl.multiple_of(group * 64, 64)
        load = lambda k: raw[pl.ds(first + k, 8, stride=ROWS), :]
        cell = group * 8 + lax.broadcasted_iota(i32, (8, LANES), 0)
        cell_x = sum((cell >= n * ext_y * ext_z).astype(i32) for n in range(1, cells_x + 1))
        rest = cell - cell_x * (ext_y * ext_z)
        cell_y = sum((rest >= n * ext_z).astype(i32) for n in range(1, cells_y + 1))
        cell_z = rest - cell_y * ext_z
        code = load(5).astype(i32)
        off_x = (code >> 9) - 1 + (cell_x >= cells_x).astype(i32)
        off_y = ((code >> 7) & 3) - 1 + (cell_y >= cells_y).astype(i32)
        off_z = ((code >> 5) & 3) - 1 + (cell_z >= cells_z).astype(i32)
        lanes = (((coord_z + off_z) & (wide_z - 1)) * SEGMENT) + (code & (SEGMENT - 1))
        near = (((off_x + coords[3]) & (wide_x - 1)) ^ coords[4]) * wide_y + (
            ((off_y + coords[5]) & (wide_y - 1)) ^ coords[6]
        )
        lane_at[pl.ds(pl.multiple_of(group * 8, 8), 8), :] = lanes
        chunk_at[pl.ds(pl.multiple_of(group * 8, 8), 8), :] = (
            (off_x + coord_x) & (wide_x - 1)
        ) * wide_y + ((off_y + coord_y) & (wide_y - 1))
        pose = [
            lookup(lambda n, k=k: table[n * POSE_ROWS + k : n * POSE_ROWS + k + 1, :], lanes, near, chunks)
            for k in range(12)
        ]
        local = [load(k) for k in range(3)]
        cell_at = (cell_x, cell_y, cell_z)
        extents = (cells_x, cells_y, cells_z)
        for k in range(3):
            arm = pose[3 * k] * local[0] + pose[3 * k + 1] * local[1] + pose[3 * k + 2] * local[2]
            arms[k, pl.ds(pl.multiple_of(group * 8, 8), 8), :] = arm
            box = float(extents[k] * (count_x, count_y, count_z)[k])
            corner = ((coord_x, coord_y, coord_z)[k] * extents[k]).astype(f32)
            middle = cell_at[k].astype(f32) + 0.5
            inside = arm + pose[9 + k] - corner - middle
            inside = inside - box * jnp.floor(inside * (1.0 / box) + 0.5)
            pos[pl.ds(first + k, 8, stride=ROWS), :] = (inside + middle) * SCALE
        radius = load(4) * SCALE
        pos[pl.ds(first + 3, 8, stride=ROWS), :] = radius
        pos[pl.ds(first + 4, 8, stride=ROWS), :] = load(3) * CHARGE_SCALE * jnp.exp2(-radius)
        return carry

    for k in range(5, ROWS):
        for group in range(padded // 8):
            pos[pl.ds(group * 64 + k, 8, stride=ROWS), :] = jnp.zeros((8, LANES), f32)
    lax.fori_loop(0, padded // 8, place, 0)
    for block in range(padded // 16):
        span = slice(block * LANES, (block + 1) * LANES)
        columns[span, :] = pos[span, :].T
        moved[span, :] = jnp.zeros((LANES, LANES), f32)
    row_force[...] = jnp.zeros(row_force.shape, f32)

    lane = lax.broadcasted_iota(i32, (8, LANES), 1)
    step_x, step_y, step_z = ext_y * ext_z, ext_z, 1
    groups = (
        (0, (0, step_x, step_y, step_z, step_x + step_y, step_x + step_z, step_y + step_z, step_x + step_y + step_z), 1),
        (step_x, (step_y, step_y + step_z), 4),
        (step_y, (step_z, step_x + step_z), 4),
        (step_z, (step_x, step_x + step_y), 4),
    )

    def visit(base, carry):
        x = base // (cells_y * cells_z)
        y = base // cells_z % cells_y
        cell = at(x, y, base % cells_z)
        for column_step, row_steps, together in groups:
            column_cell = cell + column_step
            block_at = (column_cell // 16) * LANES
            lane_base = (column_cell % 16) * ROWS
            tiles = (held[column_cell] + (8 * together - 1)) // (8 * together)

            def tile_pairs(tile, inner):
                ats, cols = [], []
                for n in range(together):
                    start = pl.multiple_of(block_at + (tile * together + n) * 8, 8)
                    packed = columns[pl.ds(start, 8), :]
                    ats.append(start)
                    cols.append(
                        [
                            jnp.take_along_axis(packed, jnp.full((8, LANES), lane_base + k, i32), axis=1)
                            for k in range(5)
                        ]
                    )
                sums = [[None] * 3 for _ in range(together)]
                for row_step in row_steps:
                    row_cell = cell + row_step
                    row = [
                        jnp.broadcast_to(pos[pl.ds(row_cell * ROWS + k, 1), :], (8, LANES)) for k in range(5)
                    ]
                    back = [None] * 3
                    for n in range(together):
                        parts = pair_terms(cols[n], row, min_reach * SCALE)
                        for k in range(3):
                            sums[n][k] = parts[k] if sums[n][k] is None else sums[n][k] + parts[k]
                            back[k] = parts[k] if back[k] is None else back[k] + parts[k]
                    if row_step != column_step:
                        span = pl.ds(pl.multiple_of(row_cell * ROWS, 8), 8)
                        for k in range(3):
                            row_force[k, span, :] = row_force[k, span, :] - back[k]
                for n in range(together):
                    span = pl.ds(ats[n], 8)
                    total = moved[span, :]
                    for k in range(3):
                        whole = jnp.sum(sums[n][k], axis=1, keepdims=True)
                        total = total + jnp.where(lane == lane_base + k, whole, 0.0)
                    moved[span, :] = total
                return inner

            lax.fori_loop(0, tiles, tile_pairs, 0)
        return carry

    lax.fori_loop(0, cells_x * cells_y * cells_z, visit, 0)

    for block in range(padded // 16):
        span = slice(block * LANES, (block + 1) * LANES)
        column_force[span, :] = moved[span, :].T

    def twist(group, carry):
        first = pl.multiple_of(group * 64, 64)
        span = pl.ds(pl.multiple_of(group * 8, 8), 8)
        force = []
        for k in range(3):
            total = column_force[pl.ds(first + k, 8, stride=ROWS), :]
            for n in range(8):
                total = total + row_force[k, pl.ds(first + n, 8, stride=ROWS), :]
            force.append(total * (clash_gain / SCALE))
        arm = [arms[k, span, :] for k in range(3)]
        rows = force + [
            arm[1] * force[2] - arm[2] * force[1],
            arm[2] * force[0] - arm[0] * force[2],
            arm[0] * force[1] - arm[1] * force[0],
        ]
        for k, value in enumerate(rows):
            contrib[pl.ds(first + k, 8, stride=ROWS), :] = value
        for k in (6, 7):
            contrib[pl.ds(first + k, 8, stride=ROWS), :] = jnp.zeros((8, LANES), f32)
        return carry

    lax.fori_loop(0, padded // 8, twist, 0)

    body = lax.broadcasted_iota(i32, (LANES, LANES), 0)

    def gather_sums(cell, total):
        value = contrib[pl.ds(pl.multiple_of(cell * ROWS, 8), 8), :]
        high = value.astype(jnp.bfloat16).astype(f32)
        low = value - high
        owner = jnp.broadcast_to(chunk_at[pl.ds(cell, 1), :], (8, LANES))
        member = jnp.broadcast_to(lane_at[pl.ds(cell, 1), :], (LANES, LANES)) == body
        pieces = []
        for chunk in range(chunks):
            mine = owner == chunk
            pieces.append(jnp.where(mine, high, 0.0))
            pieces.append(jnp.where(mine, low, 0.0))
        left = jnp.concatenate(pieces, axis=0).astype(jnp.bfloat16)
        right = jnp.where(member, 1.0, 0.0).astype(jnp.bfloat16)
        return total + lax.dot_general(left, right, (((1,), (1,)), ((), ())), preferred_element_type=f32)

    total = lax.fori_loop(0, cells, gather_sums, jnp.zeros((chunks * 16, LANES), f32))
    for chunk in range(chunks):
        out[chunk * 8 : chunk * 8 + 8, :] = total[chunk * 16 : chunk * 16 + 8] + total[chunk * 16 + 8 : chunk * 16 + 16]


def advance_rows(pose, force, torque, mobility, noise):
    centre = [pose[9 + k] + move_gain * mobility[0] * force[k] + noise[k] for k in range(3)]
    spin = [0.5 * (turn_gain * mobility[1] * torque[k] + noise[3 + k]) for k in range(3)]
    spin_sq = spin[0] * spin[0] + spin[1] * spin[1] + spin[2] * spin[2]
    factor = 2.0 / (1.0 + spin_sq)
    skew = [[None, -spin[2], spin[1]], [spin[2], None, -spin[0]], [-spin[1], spin[0], None]]
    rows = []
    for r in range(3):
        turn = []
        for c in range(3):
            inner = spin[r] * spin[c]
            turn.append(1.0 + factor * (inner - spin_sq) if r == c else factor * (skew[r][c] + inner))
        for c in range(3):
            rows.append(turn[0] * pose[c] + turn[1] * pose[3 + c] + turn[2] * pose[6 + c])
    return rows + centre


def move_kernel(sizes, coords, own, table, totals, stepped, positions, poses, fresh):
    cells_x, cells_y, cells_z, count_x, count_y, count_z, owned = sizes
    wide_x, wide_y, wide_z = window(count_x), window(count_y), window(count_z)
    chunks = wide_x * wide_y
    coord_x, coord_y, coord_z = coords[0], coords[1], coords[2]
    for x in range(wide_x):
        near_x = ((x - coord_x + coords[3]) & (wide_x - 1)) ^ coords[4]
        for y in range(wide_y):
            near_y = ((y - coord_y + coords[5]) & (wide_y - 1)) ^ coords[6]
            chunk = x * wide_y + y
            start = pl.multiple_of((near_x * wide_y + near_y) * POSE_ROWS, 8)
            poses[chunk * POSE_ROWS : (chunk + 1) * POSE_ROWS, :] = table[pl.ds(start, POSE_ROWS), :]
    for first in range(0, chunks, 8):
        many = min(8, chunks - first)
        row = [poses[pl.ds(first * POSE_ROWS + k, many, stride=POSE_ROWS), :] for k in range(20)]
        total = [totals[pl.ds(first * 8 + k, many, stride=8), :] for k in range(6)]
        new = advance_rows(row[:12], total[:3], total[3:], row[12:14], row[14:20])
        for k in range(12):
            fresh[pl.ds(first * 16 + k, many, stride=16), :] = new[k]
    mine = ((coord_x & (wide_x - 1)) * wide_y + (coord_y & (wide_y - 1))) * 16
    turned = pltpu.roll(
        fresh[pl.ds(pl.multiple_of(mine, 16), 16), :],
        LANES - (coord_z & (wide_z - 1)) * SEGMENT,
        axis=1,
    )
    stepped[...] = turned[:12, :owned]
    for first in range(0, cells_x * cells_y * cells_z, 8):
        load = lambda k: own[pl.ds(first * ROWS + k, 8, stride=ROWS), :]
        code = load(5).astype(i32)
        off_x = (code >> 9) - 1
        off_y = ((code >> 7) & 3) - 1
        off_z = ((code >> 5) & 3) - 1
        lanes = (((coord_z + off_z) & (wide_z - 1)) * SEGMENT) + (code & (SEGMENT - 1))
        chunk_at = ((off_x + coord_x) & (wide_x - 1)) * wide_y + ((off_y + coord_y) & (wide_y - 1))
        pose = [
            lookup(lambda n, k=k: fresh[n * 16 + k : n * 16 + k + 1, :], lanes, chunk_at, chunks) for k in range(12)
        ]
        local = [load(k) for k in range(3)]
        for k in range(3):
            arm = pose[3 * k] * local[0] + pose[3 * k + 1] * local[1] + pose[3 * k + 2] * local[2]
            positions[k, first : first + 8, :] = arm + pose[9 + k]


def from_offset(block, axis, distance):
    count = lax.axis_size(axis)
    return lax.ppermute(block, axis, [((i + distance) % count, i) for i in range(count)])


def from_partner(block, axis, mask):
    return lax.ppermute(block, axis, [(i ^ mask, i) for i in range(lax.axis_size(axis))])


def collect(face, poses, axis, merge):
    count = lax.axis_size(axis)
    rows = face.shape[0]
    if count == 2:
        got = from_partner(jnp.concatenate([face, poses]), axis, 1)
        return got[:rows], merge(poses, got[rows:])
    if count == 4:
        got = from_partner(jnp.concatenate([face, poses]), axis, 1)
        near, poses = got[:rows], merge(poses, got[rows:])
        got = from_partner(jnp.concatenate([near, poses]), axis, 2)
        even = lax.axis_index(axis) % 2 == 0
        return jnp.where(even, near, got[:rows]), merge(poses, got[rows:])
    got = from_offset(jnp.concatenate([face, poses]), axis, 1)
    all_poses = merge(poses, got[rows:])
    all_poses = merge(all_poses, from_offset(poses, axis, 2))
    return got[:rows], merge(all_poses, from_offset(poses, axis, -1))


def add_up(totals, axis, index):
    count = lax.axis_size(axis)
    if count <= 4:
        step = 1
        while step < count:
            totals = totals + from_partner(totals, axis, step)
            step *= 2
        return totals
    me = lax.axis_index(axis)
    owner = ((index - me + 1) & 3) - 1
    result = totals
    for distance in (-3, -2, -1, 1, 2):
        theirs = ((index - me - distance + 1) & 3) - 1
        result = result + jnp.where(theirs + distance == owner, from_offset(totals, axis, distance), 0.0)
    return result


def per_device(body_local, charges, radii, body_slot, cell_counts, poses, mobility, noise):
    cells_x, cells_y, cells_z, width = charges.shape
    owned = poses.shape[1]
    counts = tuple(lax.axis_size(axis) for axis in ("gx", "gy", "gz"))
    wide = tuple(window(count) for count in counts)
    chunks = wide[0] * wide[1]
    coord = [lax.axis_index(axis).astype(i32) for axis in ("gx", "gy", "gz")]
    turn = []
    for k in range(2):
        by_mask = coord[k] if counts[k] == 4 else jnp.zeros((), i32)
        turn += [by_mask, by_mask]
    coords = jnp.stack(coord + turn + [jnp.zeros((), i32)])
    own_cells = cells_x * cells_y * cells_z
    vmem = pl.BlockSpec(memory_space=pltpu.VMEM)
    smem = pl.BlockSpec(memory_space=pltpu.SMEM)

    own, message = pl.pallas_call(
        functools.partial(prep_kernel, (cells_x, cells_y, cells_z, owned)),
        out_shape=(
            jax.ShapeDtypeStruct((own_cells * ROWS, LANES), f32),
            jax.ShapeDtypeStruct((cells_x * cells_y * ROWS + POSE_ROWS, LANES), f32),
        ),
        in_specs=[smem, smem] + [vmem] * 7,
        out_specs=(vmem, vmem),
    )(
        jnp.stack([coord[0], coord[1], coord[2] & (wide[2] - 1)]),
        cell_counts.reshape(-1), body_local, charges, radii, body_slot, poses, mobility, noise,
    )

    def joined(first, second):
        return jnp.concatenate([first, second], axis=0)

    cell_rows = own.reshape(cells_x, cells_y, cells_z, ROWS, LANES)
    face_rows = cells_x * cells_y * ROWS
    halo_z, table = collect(message[:face_rows], message[face_rows:], "gz", jnp.add)
    high_z = halo_z.reshape(cells_x, cells_y, 1, ROWS, LANES)
    extended = jnp.concatenate([cell_rows, high_z], axis=2)
    halo_y, table = collect(extended[:, 0].reshape(-1, LANES), table, "gy", joined)
    high_y = halo_y.reshape(cells_x, 1, cells_z + 1, ROWS, LANES)
    face_x = jnp.concatenate([extended[0], high_y[0]], axis=0)
    halo_x, table = collect(face_x.reshape(-1, LANES), table, "gx", joined)

    sizes = (cells_x, cells_y, cells_z) + counts
    cells = (cells_x + 1) * (cells_y + 1) * (cells_z + 1)
    padded = -(-cells // 16) * 16
    totals = pl.pallas_call(
        functools.partial(pair_kernel, sizes),
        out_shape=jax.ShapeDtypeStruct((chunks * 8, LANES), f32),
        in_specs=[smem] + [vmem] * 5,
        out_specs=vmem,
        scratch_shapes=[
            pltpu.VMEM((padded * ROWS, LANES), f32),
            pltpu.VMEM((padded * ROWS, LANES), f32),
            pltpu.VMEM((3, padded, LANES), f32),
            pltpu.VMEM((padded, LANES), i32),
            pltpu.VMEM((padded, LANES), i32),
            pltpu.SMEM((padded,), i32),
            pltpu.VMEM((padded * ROWS, LANES), f32),
            pltpu.VMEM((3, padded * ROWS, LANES), f32),
            pltpu.VMEM((padded * ROWS, LANES), f32),
            pltpu.VMEM((padded * ROWS, LANES), f32),
            pltpu.VMEM((padded * ROWS, LANES), f32),
        ],
        compiler_params=pltpu.CompilerParams(vmem_limit_bytes=32 * 1024 * 1024),
    )(coords, own, halo_z, halo_y, halo_x, table)

    shaped = totals.reshape(wide[0], wide[1], 8, LANES)
    index_z = lax.broadcasted_iota(i32, (1, 1, 1, LANES), 3) // SEGMENT
    index_y = lax.broadcasted_iota(i32, (1, wide[1], 1, 1), 1)
    index_x = lax.broadcasted_iota(i32, (wide[0], 1, 1, 1), 0)
    shaped = add_up(shaped, "gy", index_y)
    shaped = add_up(shaped, "gx", index_x)
    shaped = add_up(shaped, "gz", index_z)

    stepped, positions = pl.pallas_call(
        functools.partial(move_kernel, sizes + (owned,)),
        out_shape=(
            jax.ShapeDtypeStruct((12, owned), f32),
            jax.ShapeDtypeStruct((3, own_cells, LANES), f32),
        ),
        in_specs=[smem] + [vmem] * 3,
        out_specs=(vmem, vmem),
        scratch_shapes=[
            pltpu.VMEM((chunks * POSE_ROWS, LANES), f32),
            pltpu.VMEM((chunks * 16, LANES), f32),
        ],
    )(coords, own, table, shaped.reshape(chunks * 8, LANES))
    return (stepped, positions.reshape(3, cells_x, cells_y, cells_z, width))


def solution(mesh):
    placed = (
        P(None, "gx", "gy", "gz", None),
        P("gx", "gy", "gz", None),
        P("gx", "gy", "gz", None),
        P("gx", "gy", "gz", None),
        P("gx", "gy", "gz"),
        P(None, ("gx", "gy", "gz")),
        P(None, ("gx", "gy", "gz")),
        P(None, ("gx", "gy", "gz")),
    )
    return jax.shard_map(
        per_device,
        mesh=mesh,
        in_specs=placed,
        out_specs=(P(None, ("gx", "gy", "gz")), P(None, "gx", "gy", "gz", None)),
        check_vma=False,
    )
```

```python
import functools
import math

import jax
import jax.numpy as jnp
from jax import lax
from jax.experimental import pallas as pl
from jax.experimental.pallas import tpu as pltpu
from jax.sharding import PartitionSpec as P

min_reach = 0.15
clash_gain = 20.0
debye_length = 0.5
move_gain = 0.02
turn_gain = 0.01

LANES = 128
ROWS = 8
POSE_ROWS = 24
SEGMENT = 32
SCALE = 1.0 / (debye_length * math.log(2.0))
CHARGE_SCALE = math.sqrt(1.0 / (clash_gain * SCALE))
EMPTY = -20.0

f32 = jnp.float32
i32 = jnp.int32

TG0, TG1 = 2, 4
SP, FO, GA = 4, 4, 8


def window(count):
    return min(count, 4)


def prep_kernel(sizes, coords, counts, local, charges, radii, slots, poses, mobility, noise, own, message):
    cells_x, cells_y, cells_z, owned = sizes
    lane = lax.broadcasted_iota(i32, (cells_z, LANES), 1)
    row = lax.broadcasted_iota(i32, (cells_z, LANES), 0)
    for x in range(cells_x):
        for y in range(cells_y):
            base = (x * cells_y + y) * cells_z * ROWS
            held = jnp.zeros((cells_z, LANES), i32)
            for z in range(cells_z):
                held = jnp.where(row == z, counts[(x * cells_y + y) * cells_z + z], held)
            filled = lane < held
            slot = slots[x, y].astype(f32)
            offset = jnp.floor((slot + 0.5) * (1.0 / owned))
            body = slot - offset * owned
            step_x = jnp.floor((offset + 0.5) * (1.0 / 9.0))
            step_y = jnp.floor((offset - 9.0 * step_x + 0.5) * (1.0 / 3.0))
            step_z = offset - 9.0 * step_x - 3.0 * step_y
            code = body + 32.0 * step_z + 128.0 * step_y + 512.0 * step_x
            rows = [
                local[0, x, y],
                local[1, x, y],
                local[2, x, y],
                jnp.where(filled, charges[x, y], 0.0),
                jnp.where(filled, radii[x, y], EMPTY / SCALE),
                code,
                held.astype(f32),
                jnp.zeros((cells_z, LANES), f32),
            ]
            for k, value in enumerate(rows):
                own[pl.ds(base + k, cells_z, stride=ROWS), :] = value
            face = (x * cells_y + y) * ROWS
            message[face : face + ROWS, :] = own[base : base + ROWS, :]
    at = cells_x * cells_y * ROWS
    message[at:, :] = jnp.zeros((POSE_ROWS, LANES), f32)
    message[at : at + 12, :owned] = poses[...]
    message[at + 12 : at + 14, :owned] = mobility[...]
    message[at + 14 : at + 20, :owned] = noise[...]
    message[at:, :] = pltpu.roll(message[at:, :], coords[2] * SEGMENT, axis=1)


def lookup(table_row, lane_at, chunk_at, chunks):
    value = None
    for chunk in range(chunks):
        row = jnp.broadcast_to(table_row(chunk), lane_at.shape)
        picked = jnp.take_along_axis(row, lane_at, axis=1)
        value = picked if value is None else jnp.where(chunk_at == chunk, picked, value)
    return value


def pair_terms(column, row, dist_floor):
    dx = column[0] - row[0]
    dy = column[1] - row[1]
    dz = column[2] - row[2]
    dist_sq = dx * dx + dy * dy + dz * dz
    inverse = lax.rsqrt(jnp.maximum(dist_sq, 1e-30))
    dist = dist_sq * inverse
    inv_reach = jnp.minimum(inverse, 1.0 / dist_floor)
    gap = (column[3] + row[3]) - dist
    cut = jnp.maximum(SCALE * SCALE - dist_sq, 0.0)
    screened = (column[4] * row[4]) * jnp.exp2(gap) * (cut * cut)
    weight = inv_reach * (jnp.maximum(gap, 0.0) + screened * ((inv_reach + math.log(2.0)) * inv_reach))
    return weight * dx, weight * dy, weight * dz


def pair_kernel(
    sizes, coords, own, halo_z, halo_y, halo_x, table, out,
    raw, pos, arms, lane_at, chunk_at, held, order, wide, row_force, column_force, contrib,
):
    cells_x, cells_y, cells_z, count_x, count_y, count_z = sizes
    wide_x, wide_y, wide_z = window(count_x), window(count_y), window(count_z)
    chunks = wide_x * wide_y
    ext_y, ext_z = cells_y + 1, cells_z + 1
    cells = (cells_x + 1) * ext_y * ext_z
    padded = raw.shape[0] // ROWS

    def at(x, y, z):
        return (x * ext_y + y) * ext_z + z

    def put(cell, ref, index):
        raw[cell * ROWS : (cell + 1) * ROWS, :] = ref[index * ROWS : (index + 1) * ROWS, :]

    for x in range(cells_x + 1):
        for y in range(ext_y):
            for z in range(ext_z):
                if x == cells_x:
                    put(at(x, y, z), halo_x, y * ext_z + z)
                elif y == cells_y:
                    put(at(x, y, z), halo_y, x * ext_z + z)
                elif z == cells_z:
                    put(at(x, y, z), halo_z, x * cells_y + y)
                else:
                    put(at(x, y, z), own, (x * cells_y + y) * cells_z + z)
    for cell in range(cells, padded):
        raw[cell * ROWS : (cell + 1) * ROWS, :] = jnp.zeros((ROWS, LANES), f32)
    for cell in range(cells):
        held[cell] = jnp.max(raw[cell * ROWS + 6 : cell * ROWS + 7, :]).astype(i32)

    coord_x, coord_y, coord_z = coords[0], coords[1], coords[2]

    def place(group, carry):
        first = pl.multiple_of(group * 64, 64)
        load = lambda k: raw[pl.ds(first + k, 8, stride=ROWS), :]
        cell = group * 8 + lax.broadcasted_iota(i32, (8, LANES), 0)
        cell_x = sum((cell >= n * ext_y * ext_z).astype(i32) for n in range(1, cells_x + 1))
        rest = cell - cell_x * (ext_y * ext_z)
        cell_y = sum((rest >= n * ext_z).astype(i32) for n in range(1, cells_y + 1))
        cell_z = rest - cell_y * ext_z
        code = load(5).astype(i32)
        off_x = (code >> 9) - 1 + (cell_x >= cells_x).astype(i32)
        off_y = ((code >> 7) & 3) - 1 + (cell_y >= cells_y).astype(i32)
        off_z = ((code >> 5) & 3) - 1 + (cell_z >= cells_z).astype(i32)
        lanes = (((coord_z + off_z) & (wide_z - 1)) * SEGMENT) + (code & (SEGMENT - 1))
        near = (((off_x + coords[3]) & (wide_x - 1)) ^ coords[4]) * wide_y + (
            ((off_y + coords[5]) & (wide_y - 1)) ^ coords[6]
        )
        lane_at[pl.ds(pl.multiple_of(group * 8, 8), 8), :] = lanes
        chunk_at[pl.ds(pl.multiple_of(group * 8, 8), 8), :] = (
            (off_x + coord_x) & (wide_x - 1)
        ) * wide_y + ((off_y + coord_y) & (wide_y - 1))
        pose = [
            lookup(lambda n, k=k: table[n * POSE_ROWS + k : n * POSE_ROWS + k + 1, :], lanes, near, chunks)
            for k in range(12)
        ]
        local = [load(k) for k in range(3)]
        cell_at = (cell_x, cell_y, cell_z)
        extents = (cells_x, cells_y, cells_z)
        for k in range(3):
            arm = pose[3 * k] * local[0] + pose[3 * k + 1] * local[1] + pose[3 * k + 2] * local[2]
            arms[k, pl.ds(pl.multiple_of(group * 8, 8), 8), :] = arm
            box = float(extents[k] * (count_x, count_y, count_z)[k])
            corner = ((coord_x, coord_y, coord_z)[k] * extents[k]).astype(f32)
            middle = cell_at[k].astype(f32) + 0.5
            inside = arm + pose[9 + k] - corner - middle
            inside = inside - box * jnp.floor(inside * (1.0 / box) + 0.5)
            pos[pl.ds(first + k, 8, stride=ROWS), :] = (inside + middle) * SCALE
        radius = load(4) * SCALE
        pos[pl.ds(first + 3, 8, stride=ROWS), :] = radius
        pos[pl.ds(first + 4, 8, stride=ROWS), :] = load(3) * CHARGE_SCALE * jnp.exp2(-radius)
        return carry

    for k in range(5, ROWS):
        for group in range(padded // 8):
            pos[pl.ds(group * 64 + k, 8, stride=ROWS), :] = jnp.zeros((8, LANES), f32)
    lax.fori_loop(0, padded // 8, place, 0)
    row_force[...] = jnp.zeros(row_force.shape, f32)
    listed = [
        at(x, y, z)
        for x in range(cells_x + 1)
        for y in range(ext_y)
        for z in range(ext_z)
        if (x == cells_x) + (y == cells_y) + (z == cells_z) < 2
    ]
    for n, cell in enumerate(listed):
        order[n] = cell
    kind = lax.broadcasted_iota(i32, (32, 5 * LANES), 1) // LANES
    part = lax.broadcasted_iota(i32, (32, 5 * LANES), 0)
    picker = jnp.where((part % 8 == kind) & (part < 24), 1.0, 0.0).astype(jnp.bfloat16)

    def spread(step, carry):
        for n in range(SP):
            cell = order[step * SP + n]
            value = pos[pl.ds(pl.multiple_of(cell * ROWS, 8), 8), :]
            high = value.astype(jnp.bfloat16).astype(f32)
            rest = value - high
            middle = rest.astype(jnp.bfloat16).astype(f32)
            low = rest - middle
            parts = jnp.concatenate([high, middle, low, jnp.zeros_like(low)], axis=0).astype(jnp.bfloat16)
            out_wide = lax.dot_general(parts, picker, (((0,), (0,)), ((), ())), preferred_element_type=f32)
            for k in range(5):
                wide[cell, k, :, :] = out_wide[:, k * LANES : (k + 1) * LANES]
        return carry

    assert len(listed) % SP == 0 and len(listed) % FO == 0
    lax.fori_loop(0, len(listed) // SP, spread, 0)

    step_x, step_y, step_z = ext_y * ext_z, ext_z, 1
    groups = (
        (0, (0, step_x, step_y, step_z, step_x + step_y, step_x + step_z, step_y + step_z, step_x + step_y + step_z), TG0),
        (step_x, (step_y, step_y + step_z), TG1),
        (step_y, (step_z, step_x + step_z), TG1),
        (step_z, (step_x, step_x + step_y), TG1),
    )

    def visit(group, base, carry):
        x = base // (cells_y * cells_z)
        y = base // cells_z % cells_y
        z = base % cells_z
        cell = at(x, y, z)
        column_step, row_steps, together = groups[group]
        column_cell = cell + column_step
        tiles = (held[column_cell] + (8 * together - 1)) // (8 * together)
        if group:
            fresh_cell = ((x, y, z)[group - 1] == (cells_x, cells_y, cells_z)[group - 1] - 1)

        def tile_pairs(tile, inner):
            spans, cols = [], []
            for n in range(together):
                span = pl.ds(pl.multiple_of((tile * together + n) * 8, 8), 8)
                spans.append(span)
                cols.append([wide[column_cell, k, span, :] for k in range(5)])
            sums = [[None] * 3 for _ in range(together)]
            for row_step in row_steps:
                row_cell = cell + row_step
                row = [
                    jnp.broadcast_to(pos[pl.ds(row_cell * ROWS + k, 1), :], (8, LANES)) for k in range(5)
                ]
                back = [None] * 3
                for n in range(together):
                    parts = pair_terms(cols[n], row, min_reach * SCALE)
                    for k in range(3):
                        sums[n][k] = parts[k] if sums[n][k] is None else sums[n][k] + parts[k]
                        back[k] = parts[k] if back[k] is None else back[k] + parts[k]
                if row_step != column_step:
                    span = pl.ds(pl.multiple_of(row_cell * ROWS, 8), 8)
                    for k in range(3):
                        row_force[k, span, :] = row_force[k, span, :] - back[k]
            for n in range(together):
                for k in range(3):
                    total = sums[n][k]
                    if group:
                        total = total + jnp.where(fresh_cell, 0.0, column_force[column_cell, k, spans[n], :])
                    column_force[column_cell, k, spans[n], :] = total
            return inner

        lax.fori_loop(0, tiles, tile_pairs, 0)
        return carry

    for group in range(len(groups)):
        lax.fori_loop(0, cells_x * cells_y * cells_z, functools.partial(visit, group), 0)

    ones = jnp.where(lax.broadcasted_iota(i32, (16, 2 * LANES), 0) == 0, 1.0, 0.0).astype(jnp.bfloat16)

    def fold(step, carry):
        lines = []
        for n in range(FO):
            cell = order[step * FO + n]
            value = column_force[cell].reshape(3 * LANES, LANES)
            high = value.astype(jnp.bfloat16)
            low = (value - high.astype(f32)).astype(jnp.bfloat16)
            both = jnp.concatenate([high, low], axis=1)
            lines.append(lax.dot_general(ones, both, (((1,), (1,)), ((), ())), preferred_element_type=f32))
        for n in range(FO):
            span = pl.ds(pl.multiple_of(order[step * FO + n] * ROWS, 8), 8)
            for k in range(3):
                row_force[k, span, :] += lines[n][:8, k * LANES : (k + 1) * LANES]
        return carry

    lax.fori_loop(0, len(listed) // FO, fold, 0)

    def twist(group, carry):
        first = pl.multiple_of(group * 64, 64)
        span = pl.ds(pl.multiple_of(group * 8, 8), 8)
        force = []
        filled = lax.broadcasted_iota(i32, (8, LANES), 1).astype(f32) < raw[pl.ds(first + 6, 8, stride=ROWS), :]
        for k in range(3):
            total = row_force[k, pl.ds(first, 8, stride=ROWS), :]
            for n in range(1, 8):
                total = total + row_force[k, pl.ds(first + n, 8, stride=ROWS), :]
            force.append(jnp.where(filled, total * (clash_gain / SCALE), 0.0))
        arm = [arms[k, span, :] for k in range(3)]
        rows = force + [
            arm[1] * force[2] - arm[2] * force[1],
            arm[2] * force[0] - arm[0] * force[2],
            arm[0] * force[1] - arm[1] * force[0],
        ]
        for k, value in enumerate(rows):
            contrib[pl.ds(first + k, 8, stride=ROWS), :] = value
        for k in (6, 7):
            contrib[pl.ds(first + k, 8, stride=ROWS), :] = jnp.zeros((8, LANES), f32)
        return carry

    lax.fori_loop(0, padded // 8, twist, 0)

    body = lax.broadcasted_iota(i32, (LANES, LANES), 0)

    def gather_sums(step, total):
        lefts, rights = [], []
        for n in range(GA):
            cell = step * GA + n
            value = contrib[pl.ds(pl.multiple_of(cell * ROWS, 8), 8), :]
            high = value.astype(jnp.bfloat16).astype(f32)
            low = value - high
            owner = jnp.broadcast_to(chunk_at[pl.ds(cell, 1), :], (8, LANES))
            member = jnp.broadcast_to(lane_at[pl.ds(cell, 1), :], (LANES, LANES)) == body
            pieces = []
            for chunk in range(chunks):
                mine = owner == chunk
                pieces.append(jnp.where(mine, high, 0.0))
                pieces.append(jnp.where(mine, low, 0.0))
            lefts.append(jnp.concatenate(pieces, axis=0).astype(jnp.bfloat16))
            rights.append(jnp.where(member, 1.0, 0.0).astype(jnp.bfloat16))
        left = jnp.concatenate(lefts, axis=1)
        right = jnp.concatenate(rights, axis=1)
        return total + lax.dot_general(left, right, (((1,), (1,)), ((), ())), preferred_element_type=f32)

    total = lax.fori_loop(0, padded // GA, gather_sums, jnp.zeros((chunks * 16, LANES), f32))
    for chunk in range(chunks):
        out[chunk * 8 : chunk * 8 + 8, :] = total[chunk * 16 : chunk * 16 + 8] + total[chunk * 16 + 8 : chunk * 16 + 16]


def advance_rows(pose, force, torque, mobility, noise):
    centre = [pose[9 + k] + move_gain * mobility[0] * force[k] + noise[k] for k in range(3)]
    spin = [0.5 * (turn_gain * mobility[1] * torque[k] + noise[3 + k]) for k in range(3)]
    spin_sq = spin[0] * spin[0] + spin[1] * spin[1] + spin[2] * spin[2]
    factor = 2.0 / (1.0 + spin_sq)
    skew = [[None, -spin[2], spin[1]], [spin[2], None, -spin[0]], [-spin[1], spin[0], None]]
    rows = []
    for r in range(3):
        turn = []
        for c in range(3):
            inner = spin[r] * spin[c]
            turn.append(1.0 + factor * (inner - spin_sq) if r == c else factor * (skew[r][c] + inner))
        for c in range(3):
            rows.append(turn[0] * pose[c] + turn[1] * pose[3 + c] + turn[2] * pose[6 + c])
    return rows + centre


def move_kernel(sizes, coords, own, table, totals, stepped, positions, poses, fresh):
    cells_x, cells_y, cells_z, count_x, count_y, count_z, owned = sizes
    wide_x, wide_y, wide_z = window(count_x), window(count_y), window(count_z)
    chunks = wide_x * wide_y
    coord_x, coord_y, coord_z = coords[0], coords[1], coords[2]
    for x in range(wide_x):
        near_x = ((x - coord_x + coords[3]) & (wide_x - 1)) ^ coords[4]
        for y in range(wide_y):
            near_y = ((y - coord_y + coords[5]) & (wide_y - 1)) ^ coords[6]
            chunk = x * wide_y + y
            start = pl.multiple_of((near_x * wide_y + near_y) * POSE_ROWS, 8)
            poses[chunk * POSE_ROWS : (chunk + 1) * POSE_ROWS, :] = table[pl.ds(start, POSE_ROWS), :]
    for first in range(0, chunks, 8):
        many = min(8, chunks - first)
        row = [poses[pl.ds(first * POSE_ROWS + k, many, stride=POSE_ROWS), :] for k in range(20)]
        total = [totals[pl.ds(first * 8 + k, many, stride=8), :] for k in range(6)]
        new = advance_rows(row[:12], total[:3], total[3:], row[12:14], row[14:20])
        for k in range(12):
            fresh[pl.ds(first * 16 + k, many, stride=16), :] = new[k]
    mine = ((coord_x & (wide_x - 1)) * wide_y + (coord_y & (wide_y - 1))) * 16
    turned = pltpu.roll(
        fresh[pl.ds(pl.multiple_of(mine, 16), 16), :],
        LANES - (coord_z & (wide_z - 1)) * SEGMENT,
        axis=1,
    )
    stepped[...] = turned[:12, :owned]
    for first in range(0, cells_x * cells_y * cells_z, 8):
        load = lambda k: own[pl.ds(first * ROWS + k, 8, stride=ROWS), :]
        code = load(5).astype(i32)
        off_x = (code >> 9) - 1
        off_y = ((code >> 7) & 3) - 1
        off_z = ((code >> 5) & 3) - 1
        lanes = (((coord_z + off_z) & (wide_z - 1)) * SEGMENT) + (code & (SEGMENT - 1))
        chunk_at = ((off_x + coord_x) & (wide_x - 1)) * wide_y + ((off_y + coord_y) & (wide_y - 1))
        pose = [
            lookup(lambda n, k=k: fresh[n * 16 + k : n * 16 + k + 1, :], lanes, chunk_at, chunks) for k in range(12)
        ]
        local = [load(k) for k in range(3)]
        for k in range(3):
            arm = pose[3 * k] * local[0] + pose[3 * k + 1] * local[1] + pose[3 * k + 2] * local[2]
            positions[k, first : first + 8, :] = arm + pose[9 + k]


def pair_sums(sizes, coords, own, halo_z, halo_y, halo_x, table):
    cells_x, cells_y, cells_z = sizes[:3]
    chunks = window(sizes[3]) * window(sizes[4])
    vmem = pl.BlockSpec(memory_space=pltpu.VMEM)
    smem = pl.BlockSpec(memory_space=pltpu.SMEM)
    cells = (cells_x + 1) * (cells_y + 1) * (cells_z + 1)
    padded = -(-cells // 16) * 16
    return pl.pallas_call(
        functools.partial(pair_kernel, sizes),
        out_shape=jax.ShapeDtypeStruct((chunks * 8, LANES), f32),
        in_specs=[smem] + [vmem] * 5,
        out_specs=vmem,
        scratch_shapes=[
            pltpu.VMEM((padded * ROWS, LANES), f32),
            pltpu.VMEM((padded * ROWS, LANES), f32),
            pltpu.VMEM((3, padded, LANES), f32),
            pltpu.VMEM((padded, LANES), i32),
            pltpu.VMEM((padded, LANES), i32),
            pltpu.SMEM((padded,), i32),
            pltpu.SMEM((padded,), i32),
            pltpu.VMEM((cells, 5, LANES, LANES), f32),
            pltpu.VMEM((3, padded * ROWS, LANES), f32),
            pltpu.VMEM((cells, 3, LANES, LANES), f32),
            pltpu.VMEM((padded * ROWS, LANES), f32),
        ],
        compiler_params=pltpu.CompilerParams(vmem_limit_bytes=48 * 1024 * 1024),
    )(coords, own, halo_z, halo_y, halo_x, table)


def from_offset(block, axis, distance):
    count = lax.axis_size(axis)
    return lax.ppermute(block, axis, [((i + distance) % count, i) for i in range(count)])


def from_partner(block, axis, mask):
    return lax.ppermute(block, axis, [(i ^ mask, i) for i in range(lax.axis_size(axis))])


def collect(face, poses, axis, merge):
    count = lax.axis_size(axis)
    rows = face.shape[0]
    if count == 2:
        got = from_partner(jnp.concatenate([face, poses]), axis, 1)
        return got[:rows], merge(poses, got[rows:])
    if count == 4:
        got = from_partner(jnp.concatenate([face, poses]), axis, 1)
        near, poses = got[:rows], merge(poses, got[rows:])
        got = from_partner(jnp.concatenate([near, poses]), axis, 2)
        even = lax.axis_index(axis) % 2 == 0
        return jnp.where(even, near, got[:rows]), merge(poses, got[rows:])
    got = from_offset(jnp.concatenate([face, poses]), axis, 1)
    all_poses = merge(poses, got[rows:])
    all_poses = merge(all_poses, from_offset(poses, axis, 2))
    return got[:rows], merge(all_poses, from_offset(poses, axis, -1))


def add_up(totals, axis, index):
    count = lax.axis_size(axis)
    if count <= 4:
        step = 1
        while step < count:
            totals = totals + from_partner(totals, axis, step)
            step *= 2
        return totals
    me = lax.axis_index(axis)
    owner = ((index - me + 1) & 3) - 1
    result = totals
    for distance in (-3, -2, -1, 1, 2):
        theirs = ((index - me - distance + 1) & 3) - 1
        result = result + jnp.where(theirs + distance == owner, from_offset(totals, axis, distance), 0.0)
    return result


def per_device(body_local, charges, radii, body_slot, cell_counts, poses, mobility, noise):
    cells_x, cells_y, cells_z, width = charges.shape
    owned = poses.shape[1]
    counts = tuple(lax.axis_size(axis) for axis in ("gx", "gy", "gz"))
    wide = tuple(window(count) for count in counts)
    chunks = wide[0] * wide[1]
    coord = [lax.axis_index(axis).astype(i32) for axis in ("gx", "gy", "gz")]
    turn = []
    for k in range(2):
        by_mask = coord[k] if counts[k] == 4 else jnp.zeros((), i32)
        turn += [by_mask, by_mask]
    coords = jnp.stack(coord + turn + [jnp.zeros((), i32)])
    own_cells = cells_x * cells_y * cells_z
    vmem = pl.BlockSpec(memory_space=pltpu.VMEM)
    smem = pl.BlockSpec(memory_space=pltpu.SMEM)

    own, message = pl.pallas_call(
        functools.partial(prep_kernel, (cells_x, cells_y, cells_z, owned)),
        out_shape=(
            jax.ShapeDtypeStruct((own_cells * ROWS, LANES), f32),
            jax.ShapeDtypeStruct((cells_x * cells_y * ROWS + POSE_ROWS, LANES), f32),
        ),
        in_specs=[smem, smem] + [vmem] * 7,
        out_specs=(vmem, vmem),
    )(
        jnp.stack([coord[0], coord[1], coord[2] & (wide[2] - 1)]),
        cell_counts.reshape(-1), body_local, charges, radii, body_slot, poses, mobility, noise,
    )

    def joined(first, second):
        return jnp.concatenate([first, second], axis=0)

    cell_rows = own.reshape(cells_x, cells_y, cells_z, ROWS, LANES)
    face_rows = cells_x * cells_y * ROWS
    halo_z, table = collect(message[:face_rows], message[face_rows:], "gz", jnp.add)
    high_z = halo_z.reshape(cells_x, cells_y, 1, ROWS, LANES)
    extended = jnp.concatenate([cell_rows, high_z], axis=2)
    halo_y, table = collect(extended[:, 0].reshape(-1, LANES), table, "gy", joined)
    high_y = halo_y.reshape(cells_x, 1, cells_z + 1, ROWS, LANES)
    face_x = jnp.concatenate([extended[0], high_y[0]], axis=0)
    halo_x, table = collect(face_x.reshape(-1, LANES), table, "gx", joined)

    sizes = (cells_x, cells_y, cells_z) + counts
    totals = pair_sums(sizes, coords, own, halo_z, halo_y, halo_x, table)

    shaped = totals.reshape(wide[0], wide[1], 8, LANES)
    index_z = lax.broadcasted_iota(i32, (1, 1, 1, LANES), 3) // SEGMENT
    index_y = lax.broadcasted_iota(i32, (1, wide[1], 1, 1), 1)
    index_x = lax.broadcasted_iota(i32, (wide[0], 1, 1, 1), 0)
    shaped = add_up(shaped, "gy", index_y)
    shaped = add_up(shaped, "gx", index_x)
    shaped = add_up(shaped, "gz", index_z)

    stepped, positions = pl.pallas_call(
        functools.partial(move_kernel, sizes + (owned,)),
        out_shape=(
            jax.ShapeDtypeStruct((12, owned), f32),
            jax.ShapeDtypeStruct((3, own_cells, LANES), f32),
        ),
        in_specs=[smem] + [vmem] * 3,
        out_specs=(vmem, vmem),
        scratch_shapes=[
            pltpu.VMEM((chunks * POSE_ROWS, LANES), f32),
            pltpu.VMEM((chunks * 16, LANES), f32),
        ],
    )(coords, own, table, shaped.reshape(chunks * 8, LANES))
    return (stepped, positions.reshape(3, cells_x, cells_y, cells_z, width))


def solution(mesh):
    placed = (
        P(None, "gx", "gy", "gz", None),
        P("gx", "gy", "gz", None),
        P("gx", "gy", "gz", None),
        P("gx", "gy", "gz", None),
        P("gx", "gy", "gz"),
        P(None, ("gx", "gy", "gz")),
        P(None, ("gx", "gy", "gz")),
        P(None, ("gx", "gy", "gz")),
    )
    return jax.shard_map(
        per_device,
        mesh=mesh,
        in_specs=placed,
        out_specs=(P(None, ("gx", "gy", "gz")), P(None, "gx", "gy", "gz", None)),
        check_vma=False,
    )
```

```python
import functools
import itertools
import math

import jax
import jax.numpy as jnp
from jax import lax
from jax.experimental import pallas as pl
from jax.experimental.pallas import tpu as pltpu
from jax.sharding import PartitionSpec as P

min_reach = 0.15
clash_gain = 20.0
debye_length = 0.5
move_gain = 0.02
turn_gain = 0.01

LANES = 128
ROWS = 8
BODY_ROWS = 20
PACKED = 4
SEGMENT = 32
SCALE = 1.0 / (debye_length * math.log(2.0))
CHARGE_SCALE = math.sqrt(1.0 / (clash_gain * SCALE))
EMPTY = -20.0

f32 = jnp.float32
i32 = jnp.int32

T_ALL = (4, 4, 4, 4, 4, 4, 2, 2, 2, 2, 2, 2)
SP, FO, GA = 4, 4, 8
HALO_ORDER = (1, 0, 2)


def unpack(packed, owned, spread_rows, table):
    per_row = BODY_ROWS // PACKED
    row = lax.broadcasted_iota(i32, (8, LANES), 0)
    lane = lax.broadcasted_iota(i32, (8, LANES), 1)
    for first in range(0, packed.shape[0], 8):
        value = packed[first : first + 8, :]
        segment = ((first + row) // PACKED) % 4
        inside = lane - segment * SEGMENT
        valid = (inside >= 0) & (inside < owned)
        for j in range(per_row):
            index = jnp.where(valid, inside + j * owned, 0)
            picked = jnp.take_along_axis(value, index, axis=1)
            spread_rows[j, first : first + 8, :] = jnp.where(valid, picked, 0.0)
    chunks = table.shape[1]
    for m in range(BODY_ROWS):
        for first in range(0, chunks, 8):
            many = min(8, chunks - first)
            parts = [
                spread_rows[m % per_row, pl.ds((first * 4 + c) * PACKED + m // per_row, many, stride=4 * PACKED), :]
                for c in range(4)
            ]
            table[m, first : first + many, :] = (parts[0] + parts[1]) + (parts[2] + parts[3])


def owner_at(code, coords, counts, beyond=(0, 0, 0)):
    steps = ((code >> 9) - 1, ((code >> 7) & 3) - 1, ((code >> 5) & 3) - 1)
    x, y, z = [(step + coords[k] + beyond[k]) & (counts[k] - 1) for k, step in enumerate(steps)]
    chunk = (x * counts[1] + y) * (counts[2] // 4) + (z >> 2)
    return chunk, (z & 3) * SEGMENT + (code & (SEGMENT - 1))


def prep_kernel(sizes, axis, counts, local, charges, radii, slots, poses, mobility, noise, own, face, bodies, rows):
    cells_x, cells_y, cells_z, owned = sizes
    per_row = BODY_ROWS // PACKED
    rows[...] = jnp.zeros(rows.shape, f32)
    rows[0:12, :owned] = poses[...]
    rows[12:14, :owned] = mobility[...]
    rows[14:20, :owned] = noise[...]
    packed = rows[pl.ds(0, PACKED, stride=per_row), :]
    for j in range(1, per_row):
        packed = packed + pltpu.roll(rows[pl.ds(j, PACKED, stride=per_row), :], j * owned, axis=1)
    for device in range(bodies.shape[0]):
        bodies[device] = packed
    lane = lax.broadcasted_iota(i32, (cells_z, LANES), 1)
    row = lax.broadcasted_iota(i32, (cells_z, LANES), 0)
    for x in range(cells_x):
        for y in range(cells_y):
            base = (x * cells_y + y) * cells_z * ROWS
            held = jnp.zeros((cells_z, LANES), i32)
            for z in range(cells_z):
                held = jnp.where(row == z, counts[x, y, z], held)
            filled = lane < held
            slot = slots[x, y].astype(f32)
            offset = jnp.floor((slot + 0.5) * (1.0 / owned))
            body = slot - offset * owned
            step_x = jnp.floor((offset + 0.5) * (1.0 / 9.0))
            step_y = jnp.floor((offset - 9.0 * step_x + 0.5) * (1.0 / 3.0))
            step_z = offset - 9.0 * step_x - 3.0 * step_y
            code = body + 32.0 * step_z + 128.0 * step_y + 512.0 * step_x
            rows = [
                local[0, x, y],
                local[1, x, y],
                local[2, x, y],
                jnp.where(filled, charges[x, y], 0.0),
                jnp.where(filled, radii[x, y], EMPTY / SCALE),
                code,
                held.astype(f32),
                jnp.zeros((cells_z, LANES), f32),
            ]
            for k, value in enumerate(rows):
                own[pl.ds(base + k, cells_z, stride=ROWS), :] = value
    at = 0
    for x in range(1 if axis == 0 else cells_x):
        for y in range(1 if axis == 1 else cells_y):
            for z in range(1 if axis == 2 else cells_z):
                base = ((x * cells_y + y) * cells_z + z) * ROWS
                face[at : at + ROWS, :] = own[base : base + ROWS, :]
                at += ROWS


def lookup(table_row, lane_at, chunk_at, chunks):
    value = None
    for chunk in range(chunks):
        row = jnp.broadcast_to(table_row(chunk), lane_at.shape)
        picked = jnp.take_along_axis(row, lane_at, axis=1)
        value = picked if value is None else jnp.where(chunk_at == chunk, picked, value)
    return value


def tiles_together(rows):
    return T_ALL[min(rows, len(T_ALL)) - 1]


@functools.cache
def pair_plan(cells_x, cells_y, cells_z):
    corners = [(x, y, z) for x in (0, 1) for y in (0, 1) for z in (0, 1)]
    kinds = [
        (low, high)
        for n, low in enumerate(corners)
        for high in corners[n:]
        if all(min(i, j) == 0 for i, j in zip(low, high))
    ]
    own = [(x, y, z) for x in range(cells_x) for y in range(cells_y) for z in range(cells_z)]
    pairs = [
        tuple(tuple(i + j for i, j in zip(base, corner)) for corner in kind) for base in own for kind in kinds
    ]
    rows = {cell: [] for cell in own}
    later = []
    for low, high in pairs:
        if low in rows and high not in rows:
            rows[low].append(high)
        elif high in rows and low not in rows:
            rows[high].append(low)
        elif low == high:
            rows[low].append(high)
        else:
            later.append((low, high))
    outside = [pair for pair in later if pair[0] not in rows]
    for low, high in later:
        if low in rows:
            short, other = sorted((low, high), key=lambda cell: (len(rows[cell]), cell))
            rows[short].append(other)
    while outside:
        names = sorted({cell for pair in outside for cell in pair})
        best = max(names, key=lambda cell: sum(cell in pair for pair in outside))
        rows[best] = [pair[1] if pair[0] == best else pair[0] for pair in outside if best in pair]
        outside = [pair for pair in outside if best not in pair]
    return tuple((cell, tuple(others)) for cell, others in rows.items())


def pair_terms(column, row, dist_floor):
    dx = column[0] - row[0]
    dy = column[1] - row[1]
    dz = column[2] - row[2]
    dist_sq = dx * dx + dy * dy + dz * dz
    inverse = lax.rsqrt(jnp.maximum(dist_sq, 1e-30))
    dist = dist_sq * inverse
    inv_reach = jnp.minimum(inverse, 1.0 / dist_floor)
    gap = (column[3] + row[3]) - dist
    cut = jnp.maximum(SCALE * SCALE - dist_sq, 0.0)
    screened = (column[4] * row[4]) * jnp.exp2(gap) * (cut * cut)
    weight = inv_reach * (jnp.maximum(gap, 0.0) + screened * ((inv_reach + math.log(2.0)) * inv_reach))
    return weight * dx, weight * dy, weight * dz


def pair_kernel(
    sizes, coords, own, first_halo, second_halo, third_halo, packed, out, table,
    spread_rows, raw, pos, arms, lane_at, chunk_at, held, order, wide, row_force, column_force, contrib,
):
    cells_x, cells_y, cells_z, count_x, count_y, count_z, owned = sizes
    chunks = table.shape[1]
    unpack(packed, owned, spread_rows, table)
    ext_y, ext_z = cells_y + 1, cells_z + 1
    cells = (cells_x + 1) * ext_y * ext_z
    padded = raw.shape[0] // ROWS

    def at(x, y, z):
        return (x * ext_y + y) * ext_z + z

    def put(cell, ref, index):
        raw[cell * ROWS : (cell + 1) * ROWS, :] = ref[index * ROWS : (index + 1) * ROWS, :]

    extents = (cells_x, cells_y, cells_z)
    halos = (first_halo, second_halo, third_halo)
    for place_at in itertools.product(*[range(extent + 1) for extent in extents]):
        source, shape = own, list(extents)
        for step, axis in enumerate(HALO_ORDER):
            if place_at[axis] == extents[axis]:
                source = halos[step]
                shape = [extent + (HALO_ORDER.index(k) < step) for k, extent in enumerate(extents)]
                shape[axis] = 1
        index = 0
        for k in range(3):
            index = index * shape[k] + (0 if shape[k] == 1 else place_at[k])
        put(at(*place_at), source, index)
    for cell in range(cells, padded):
        raw[cell * ROWS : (cell + 1) * ROWS, :] = jnp.zeros((ROWS, LANES), f32)
    for cell in range(cells):
        held[cell] = jnp.max(raw[cell * ROWS + 6 : cell * ROWS + 7, :]).astype(i32)

    coord_x, coord_y, coord_z = coords[0], coords[1], coords[2]

    def place(group, carry):
        first = pl.multiple_of(group * 64, 64)
        load = lambda k: raw[pl.ds(first + k, 8, stride=ROWS), :]
        cell = group * 8 + lax.broadcasted_iota(i32, (8, LANES), 0)
        cell_x = sum((cell >= n * ext_y * ext_z).astype(i32) for n in range(1, cells_x + 1))
        rest = cell - cell_x * (ext_y * ext_z)
        cell_y = sum((rest >= n * ext_z).astype(i32) for n in range(1, cells_y + 1))
        cell_z = rest - cell_y * ext_z
        code = load(5).astype(i32)
        beyond = [
            (cell_now >= cells_now).astype(i32)
            for cell_now, cells_now in ((cell_x, cells_x), (cell_y, cells_y), (cell_z, cells_z))
        ]
        owners, lanes = owner_at(code, (coord_x, coord_y, coord_z), (count_x, count_y, count_z), beyond)
        lane_at[pl.ds(pl.multiple_of(group * 8, 8), 8), :] = lanes
        chunk_at[pl.ds(pl.multiple_of(group * 8, 8), 8), :] = owners
        pose = [lookup(lambda n, k=k: table[k, n : n + 1, :], lanes, owners, chunks) for k in range(12)]
        local = [load(k) for k in range(3)]
        cell_at = (cell_x, cell_y, cell_z)
        extents = (cells_x, cells_y, cells_z)
        for k in range(3):
            arm = pose[3 * k] * local[0] + pose[3 * k + 1] * local[1] + pose[3 * k + 2] * local[2]
            arms[k, pl.ds(pl.multiple_of(group * 8, 8), 8), :] = arm
            box = float(extents[k] * (count_x, count_y, count_z)[k])
            corner = ((coord_x, coord_y, coord_z)[k] * extents[k]).astype(f32)
            middle = cell_at[k].astype(f32) + 0.5
            inside = arm + pose[9 + k] - corner - middle
            inside = inside - box * jnp.floor(inside * (1.0 / box) + 0.5)
            pos[pl.ds(first + k, 8, stride=ROWS), :] = (inside + middle) * SCALE
        radius = load(4) * SCALE
        pos[pl.ds(first + 3, 8, stride=ROWS), :] = radius
        pos[pl.ds(first + 4, 8, stride=ROWS), :] = load(3) * CHARGE_SCALE * jnp.exp2(-radius)
        return carry

    for k in range(5, ROWS):
        for group in range(padded // 8):
            pos[pl.ds(group * 64 + k, 8, stride=ROWS), :] = jnp.zeros((8, LANES), f32)
    lax.fori_loop(0, padded // 8, place, 0)
    row_force[...] = jnp.zeros(row_force.shape, f32)
    plan = pair_plan(cells_x, cells_y, cells_z)
    listed = [at(*column) for column, _ in plan]
    listed += [listed[-1]] * (-len(listed) % 4)
    for n, cell in enumerate(listed):
        order[n] = cell
    kind = lax.broadcasted_iota(i32, (32, 5 * LANES), 1) // LANES
    part = lax.broadcasted_iota(i32, (32, 5 * LANES), 0)
    picker = jnp.where((part % 8 == kind) & (part < 24), 1.0, 0.0).astype(jnp.bfloat16)

    def spread(step, carry):
        for n in range(SP):
            cell = order[step * SP + n]
            value = pos[pl.ds(pl.multiple_of(cell * ROWS, 8), 8), :]
            high = value.astype(jnp.bfloat16).astype(f32)
            rest = value - high
            middle = rest.astype(jnp.bfloat16).astype(f32)
            low = rest - middle
            parts = jnp.concatenate([high, middle, low, jnp.zeros_like(low)], axis=0).astype(jnp.bfloat16)
            out_wide = lax.dot_general(parts, picker, (((0,), (0,)), ((), ())), preferred_element_type=f32)
            for k in range(5):
                wide[cell, k, :, :] = out_wide[:, k * LANES : (k + 1) * LANES]
        return carry

    lax.fori_loop(0, len(listed) // SP, spread, 0)

    for column, rows in plan:
        column_cell = at(*column)
        row_cells = [at(*row) for row in rows]

        def tile_pairs(first, together, step, inner, column_cell=column_cell, row_cells=row_cells):
            spans, cols = [], []
            for n in range(together):
                span = pl.ds(pl.multiple_of((first + step * together + n) * 8, 8), 8)
                spans.append(span)
                cols.append([wide[column_cell, k, span, :] for k in range(5)])
            sums = [[None] * 3 for _ in range(together)]
            for row_cell in row_cells:
                row = [
                    jnp.broadcast_to(pos[row_cell * ROWS + k : row_cell * ROWS + k + 1, :], (8, LANES))
                    for k in range(5)
                ]
                back = [None] * 3
                for n in range(together):
                    parts = pair_terms(cols[n], row, min_reach * SCALE)
                    for k in range(3):
                        sums[n][k] = parts[k] if sums[n][k] is None else sums[n][k] + parts[k]
                        back[k] = parts[k] if back[k] is None else back[k] + parts[k]
                if row_cell != column_cell:
                    span = slice(row_cell * ROWS, row_cell * ROWS + ROWS)
                    for k in range(3):
                        row_force[k, span, :] = row_force[k, span, :] - back[k]
            for n in range(together):
                for k in range(3):
                    column_force[column_cell, k, spans[n], :] = sums[n][k]
            return inner

        tiles = (held[column_cell] + 7) // 8
        together = tiles_together(len(rows))
        whole = tiles // together
        lax.fori_loop(0, whole, functools.partial(tile_pairs, 0, together), 0)
        rest = tiles - whole * together
        if together >= 4:
            lax.fori_loop(0, (rest + 1) // 2, functools.partial(tile_pairs, whole * together, 2), 0)
        elif together > 1:
            lax.fori_loop(0, rest, functools.partial(tile_pairs, whole * together, 1), 0)

    ones = jnp.where(lax.broadcasted_iota(i32, (16, 2 * LANES), 0) == 0, 1.0, 0.0).astype(jnp.bfloat16)

    def fold_line(cell):
        value = column_force[cell].reshape(3 * LANES, LANES)
        high = value.astype(jnp.bfloat16)
        low = (value - high.astype(f32)).astype(jnp.bfloat16)
        both = jnp.concatenate([high, low], axis=1)
        return lax.dot_general(ones, both, (((1,), (1,)), ((), ())), preferred_element_type=f32)

    def fold(cells_now):
        lines = [fold_line(cell) for cell in cells_now]
        for cell, line in zip(cells_now, lines):
            span = pl.ds(pl.multiple_of(cell * ROWS, 8), 8)
            for k in range(3):
                row_force[k, span, :] += line[:8, k * LANES : (k + 1) * LANES]

    def fold_step(step, carry):
        fold([order[step * FO + n] for n in range(FO)])
        return carry

    even = len(plan) // FO
    lax.fori_loop(0, even, fold_step, 0)
    fold([order[n] for n in range(even * FO, len(plan))])

    def twist(group, carry):
        first = pl.multiple_of(group * 64, 64)
        span = pl.ds(pl.multiple_of(group * 8, 8), 8)
        force = []
        filled = lax.broadcasted_iota(i32, (8, LANES), 1).astype(f32) < raw[pl.ds(first + 6, 8, stride=ROWS), :]
        for k in range(3):
            total = row_force[k, pl.ds(first, 8, stride=ROWS), :]
            for n in range(1, 8):
                total = total + row_force[k, pl.ds(first + n, 8, stride=ROWS), :]
            force.append(jnp.where(filled, total * (clash_gain / SCALE), 0.0))
        arm = [arms[k, span, :] for k in range(3)]
        rows = force + [
            arm[1] * force[2] - arm[2] * force[1],
            arm[2] * force[0] - arm[0] * force[2],
            arm[0] * force[1] - arm[1] * force[0],
        ]
        for k, value in enumerate(rows):
            contrib[pl.ds(first + k, 8, stride=ROWS), :] = value
        for k in (6, 7):
            contrib[pl.ds(first + k, 8, stride=ROWS), :] = jnp.zeros((8, LANES), f32)
        return carry

    lax.fori_loop(0, padded // 8, twist, 0)

    body = lax.broadcasted_iota(i32, (LANES, LANES), 0)

    def gather_sums(step, total):
        lefts, rights = [], []
        for n in range(GA):
            cell = step * GA + n
            value = contrib[pl.ds(pl.multiple_of(cell * ROWS, 8), 8), :]
            high = value.astype(jnp.bfloat16).astype(f32)
            low = value - high
            owner = jnp.broadcast_to(chunk_at[pl.ds(cell, 1), :], (8, LANES))
            member = jnp.broadcast_to(lane_at[pl.ds(cell, 1), :], (LANES, LANES)) == body
            pieces = []
            for chunk in range(chunks):
                mine = owner == chunk
                pieces.append(jnp.where(mine, high, 0.0))
                pieces.append(jnp.where(mine, low, 0.0))
            lefts.append(jnp.concatenate(pieces, axis=0).astype(jnp.bfloat16))
            rights.append(jnp.where(member, 1.0, 0.0).astype(jnp.bfloat16))
        left = jnp.concatenate(lefts, axis=1)
        right = jnp.concatenate(rights, axis=1)
        return total + lax.dot_general(left, right, (((1,), (1,)), ((), ())), preferred_element_type=f32)

    total = lax.fori_loop(0, padded // GA, gather_sums, jnp.zeros((chunks * 16, LANES), f32))
    for chunk in range(chunks):
        out[chunk * 8 : chunk * 8 + 8, :] = total[chunk * 16 : chunk * 16 + 8] + total[chunk * 16 + 8 : chunk * 16 + 16]


def advance_rows(pose, force, torque, mobility, noise):
    centre = [pose[9 + k] + move_gain * mobility[0] * force[k] + noise[k] for k in range(3)]
    spin = [0.5 * (turn_gain * mobility[1] * torque[k] + noise[3 + k]) for k in range(3)]
    spin_sq = spin[0] * spin[0] + spin[1] * spin[1] + spin[2] * spin[2]
    factor = 2.0 / (1.0 + spin_sq)
    skew = [[None, -spin[2], spin[1]], [spin[2], None, -spin[0]], [-spin[1], spin[0], None]]
    rows = []
    for r in range(3):
        turn = []
        for c in range(3):
            inner = spin[r] * spin[c]
            turn.append(1.0 + factor * (inner - spin_sq) if r == c else factor * (skew[r][c] + inner))
        for c in range(3):
            rows.append(turn[0] * pose[c] + turn[1] * pose[3 + c] + turn[2] * pose[6 + c])
    return rows + centre


def move_kernel(sizes, coords, own, table, totals, others, stepped, positions, fresh):
    cells_x, cells_y, cells_z, count_x, count_y, count_z, owned = sizes
    chunks = table.shape[1]
    for first in range(0, chunks, 8):
        many = min(8, chunks - first)
        row = [table[k, first : first + many, :] for k in range(BODY_ROWS)]
        total = [
            totals[pl.ds(first * 8 + k, many, stride=8), :] + others[pl.ds(first * 8 + k, many, stride=8), :]
            for k in range(6)
        ]
        new = advance_rows(row[:12], total[:3], total[3:], row[12:14], row[14:20])
        for k in range(12):
            fresh[pl.ds(first * 16 + k, many, stride=16), :] = new[k]
    mine = ((coords[0] * count_y + coords[1]) * (count_z // 4) + (coords[2] >> 2)) * 16
    turned = pltpu.roll(
        fresh[pl.ds(pl.multiple_of(mine, 16), 16), :], (4 - (coords[2] & 3)) * SEGMENT, axis=1
    )
    stepped[...] = turned[:12, :owned]
    for first in range(0, cells_x * cells_y * cells_z, 8):
        load = lambda k: own[pl.ds(first * ROWS + k, 8, stride=ROWS), :]
        owners, lanes = owner_at(
            load(5).astype(i32), (coords[0], coords[1], coords[2]), (count_x, count_y, count_z)
        )
        pose = [
            lookup(lambda n, k=k: fresh[n * 16 + k : n * 16 + k + 1, :], lanes, owners, chunks) for k in range(12)
        ]
        local = [load(k) for k in range(3)]
        for k in range(3):
            arm = pose[3 * k] * local[0] + pose[3 * k + 1] * local[1] + pose[3 * k + 2] * local[2]
            positions[k, first : first + 8, :] = arm + pose[9 + k]


def pair_sums(sizes, coords, own, first_halo, second_halo, third_halo, packed):
    cells_x, cells_y, cells_z = sizes[:3]
    chunks = packed.shape[0] // (4 * PACKED)
    vmem = pl.BlockSpec(memory_space=pltpu.VMEM)
    smem = pl.BlockSpec(memory_space=pltpu.SMEM)
    cells = (cells_x + 1) * (cells_y + 1) * (cells_z + 1)
    padded = -(-cells // 16) * 16
    return pl.pallas_call(
        functools.partial(pair_kernel, sizes),
        out_shape=(
            jax.ShapeDtypeStruct((chunks * 8, LANES), f32),
            jax.ShapeDtypeStruct((BODY_ROWS, chunks, LANES), f32),
        ),
        in_specs=[smem] + [vmem] * 5,
        out_specs=(vmem, vmem),
        scratch_shapes=[
            pltpu.VMEM((BODY_ROWS // PACKED,) + packed.shape, f32),
            pltpu.VMEM((padded * ROWS, LANES), f32),
            pltpu.VMEM((padded * ROWS, LANES), f32),
            pltpu.VMEM((3, padded, LANES), f32),
            pltpu.VMEM((padded, LANES), i32),
            pltpu.VMEM((padded, LANES), i32),
            pltpu.SMEM((padded,), i32),
            pltpu.SMEM((padded,), i32),
            pltpu.VMEM((cells, 5, LANES, LANES), f32),
            pltpu.VMEM((3, padded * ROWS, LANES), f32),
            pltpu.VMEM((cells, 3, LANES, LANES), f32),
            pltpu.VMEM((padded * ROWS, LANES), f32),
        ],
        compiler_params=pltpu.CompilerParams(vmem_limit_bytes=48 * 1024 * 1024),
    )(coords, own, first_halo, second_halo, third_halo, packed)


def from_next(block, axis):
    count = lax.axis_size(axis)
    return lax.ppermute(block, axis, [((i + 1) % count, i) for i in range(count)])


def from_partner(block, axis, mask):
    return lax.ppermute(block, axis, [(i ^ mask, i) for i in range(lax.axis_size(axis))])


def per_device(body_local, charges, radii, body_slot, cell_counts, poses, mobility, noise):
    cells_x, cells_y, cells_z, width = charges.shape
    owned = poses.shape[1]
    axes = ("gx", "gy", "gz")
    counts = tuple(lax.axis_size(axis) for axis in axes)
    devices = math.prod(counts)
    assert owned <= SEGMENT and BODY_ROWS // PACKED * owned <= LANES and width == LANES
    assert counts[2] % 4 == 0 and all(count & (count - 1) == 0 for count in counts)
    coords = jnp.stack([lax.axis_index(axis).astype(i32) for axis in axes])
    own_cells = cells_x * cells_y * cells_z
    vmem = pl.BlockSpec(memory_space=pltpu.VMEM)
    smem = pl.BlockSpec(memory_space=pltpu.SMEM)

    first_axis = HALO_ORDER[0]
    face_cells = own_cells // (cells_x, cells_y, cells_z)[first_axis]
    own, face, bodies = pl.pallas_call(
        functools.partial(prep_kernel, (cells_x, cells_y, cells_z, owned), first_axis),
        out_shape=(
            jax.ShapeDtypeStruct((own_cells * ROWS, LANES), f32),
            jax.ShapeDtypeStruct((face_cells * ROWS, LANES), f32),
            jax.ShapeDtypeStruct((devices, PACKED, LANES), f32),
        ),
        in_specs=[smem] + [vmem] * 7,
        out_specs=(vmem, vmem, vmem),
        scratch_shapes=[pltpu.VMEM((24, LANES), f32)],
    )(cell_counts, body_local, charges, radii, body_slot, poses, mobility, noise)
    packed = lax.all_to_all(bodies, axes, 0, 0).reshape(devices * PACKED, LANES)

    extended = own.reshape(cells_x, cells_y, cells_z, ROWS, LANES)
    halos = []
    for axis in HALO_ORDER:
        shape = extended.shape[:axis] + (1,) + extended.shape[axis + 1 :]
        if halos:
            face = lax.slice_in_dim(extended, 0, 1, axis=axis).reshape(-1, LANES)
        halos.append(from_next(face, axes[axis]))
        extended = jnp.concatenate([extended, halos[-1].reshape(shape)], axis=axis)

    sizes = (cells_x, cells_y, cells_z) + counts + (owned,)
    totals, table = pair_sums(sizes, coords, own, *halos, packed)

    others = jnp.zeros_like(totals)
    for axis in ("gy", "gx", "gz"):
        step = 1
        while step < lax.axis_size(axis):
            totals = totals + others
            others = from_partner(totals, axis, step)
            step *= 2

    stepped, positions = pl.pallas_call(
        functools.partial(move_kernel, sizes),
        out_shape=(
            jax.ShapeDtypeStruct((12, owned), f32),
            jax.ShapeDtypeStruct((3, own_cells, LANES), f32),
        ),
        in_specs=[smem] + [vmem] * 4,
        out_specs=(vmem, vmem),
        scratch_shapes=[pltpu.VMEM((table.shape[1] * 16, LANES), f32)],
    )(coords, own, table, totals, others)
    return (stepped, positions.reshape(3, cells_x, cells_y, cells_z, width))


def solution(mesh):
    placed = (
        P(None, "gx", "gy", "gz", None),
        P("gx", "gy", "gz", None),
        P("gx", "gy", "gz", None),
        P("gx", "gy", "gz", None),
        P("gx", "gy", "gz"),
        P(None, ("gx", "gy", "gz")),
        P(None, ("gx", "gy", "gz")),
        P(None, ("gx", "gy", "gz")),
    )
    return jax.shard_map(
        per_device,
        mesh=mesh,
        in_specs=placed,
        out_specs=(P(None, ("gx", "gy", "gz")), P(None, "gx", "gy", "gz", None)),
        check_vma=False,
    )
```

```python
import functools
import itertools
import math

import jax
import jax.numpy as jnp
from jax import lax
from jax.experimental import pallas as pl
from jax.experimental.pallas import tpu as pltpu
from jax.sharding import PartitionSpec as P

min_reach = 0.15
clash_gain = 20.0
debye_length = 0.5
move_gain = 0.02
turn_gain = 0.01

LANES = 128
ROWS = 8
BODY_ROWS = 20
PACKED = 4
SEGMENT = 32
SCALE = 1.0 / (debye_length * math.log(2.0))
CHARGE_SCALE = math.sqrt(1.0 / (clash_gain * SCALE))
EMPTY = -20.0

f32 = jnp.float32
i32 = jnp.int32

T_ALL = (4, 4, 4, 4, 4, 4, 2, 2, 2, 2, 2, 2)
SP, FO, GA = 12, 6, 16
HALO_ORDER = (1, 0, 2)
SMALL_VMEM = 8 * 1024 * 1024
PAIR_VMEM = 24 * 1024 * 1024


def unpack(packed, owned, spread_rows, table):
    per_row = BODY_ROWS // PACKED
    row = lax.broadcasted_iota(i32, (8, LANES), 0)
    lane = lax.broadcasted_iota(i32, (8, LANES), 1)
    for first in range(0, packed.shape[0], 8):
        value = packed[first : first + 8, :]
        segment = ((first + row) // PACKED) % 4
        inside = lane - segment * SEGMENT
        valid = (inside >= 0) & (inside < owned)
        for j in range(per_row):
            index = jnp.where(valid, inside + j * owned, 0)
            picked = jnp.take_along_axis(value, index, axis=1)
            spread_rows[j, first : first + 8, :] = jnp.where(valid, picked, 0.0)
    chunks = table.shape[1]
    for m in range(BODY_ROWS):
        for first in range(0, chunks, 8):
            many = min(8, chunks - first)
            parts = [
                spread_rows[m % per_row, pl.ds((first * 4 + c) * PACKED + m // per_row, many, stride=4 * PACKED), :]
                for c in range(4)
            ]
            table[m, first : first + many, :] = (parts[0] + parts[1]) + (parts[2] + parts[3])


def owner_at(code, coords, counts, beyond=(0, 0, 0)):
    steps = ((code >> 9) - 1, ((code >> 7) & 3) - 1, ((code >> 5) & 3) - 1)
    x, y, z = [(step + coords[k] + beyond[k]) & (counts[k] - 1) for k, step in enumerate(steps)]
    chunk = (x * counts[1] + y) * (counts[2] // 4) + (z >> 2)
    return chunk, (z & 3) * SEGMENT + (code & (SEGMENT - 1))


def prep_kernel(sizes, axis, counts, local, charges, radii, slots, poses, mobility, noise, own, face, bodies, rows):
    cells_x, cells_y, cells_z, owned = sizes
    per_row = BODY_ROWS // PACKED
    rows[...] = jnp.zeros(rows.shape, f32)
    rows[0:12, :owned] = poses[...]
    rows[12:14, :owned] = mobility[...]
    rows[14:20, :owned] = noise[...]
    packed = rows[pl.ds(0, PACKED, stride=per_row), :]
    for j in range(1, per_row):
        packed = packed + pltpu.roll(rows[pl.ds(j, PACKED, stride=per_row), :], j * owned, axis=1)
    for device in range(bodies.shape[0]):
        bodies[device] = packed
    lane = lax.broadcasted_iota(i32, (cells_z, LANES), 1)
    row = lax.broadcasted_iota(i32, (cells_z, LANES), 0)
    for x in range(cells_x):
        for y in range(cells_y):
            base = (x * cells_y + y) * cells_z * ROWS
            count = jnp.zeros((cells_z, LANES), i32)
            for z in range(cells_z):
                count = jnp.where(row == z, counts[x, y, z], count)
            filled = lane < count
            slot = slots[x, y].astype(f32)
            offset = jnp.floor((slot + 0.5) * (1.0 / owned))
            body = slot - offset * owned
            step_x = jnp.floor((offset + 0.5) * (1.0 / 9.0))
            step_y = jnp.floor((offset - 9.0 * step_x + 0.5) * (1.0 / 3.0))
            step_z = offset - 9.0 * step_x - 3.0 * step_y
            code = body + 32.0 * step_z + 128.0 * step_y + 512.0 * step_x
            rows = [
                local[0, x, y],
                local[1, x, y],
                local[2, x, y],
                jnp.where(filled, charges[x, y], 0.0),
                jnp.where(filled, radii[x, y], EMPTY / SCALE),
                code,
                count.astype(f32),
                jnp.zeros((cells_z, LANES), f32),
            ]
            for k, value in enumerate(rows):
                own[pl.ds(base + k, cells_z, stride=ROWS), :] = value
    at = 0
    for x in range(1 if axis == 0 else cells_x):
        for y in range(1 if axis == 1 else cells_y):
            for z in range(1 if axis == 2 else cells_z):
                base = ((x * cells_y + y) * cells_z + z) * ROWS
                face[at : at + ROWS, :] = own[base : base + ROWS, :]
                at += ROWS


def lookup(table_row, lane_at, chunk_at, chunks):
    value = None
    for chunk in range(chunks):
        row = jnp.broadcast_to(table_row(chunk), lane_at.shape)
        picked = jnp.take_along_axis(row, lane_at, axis=1)
        value = picked if value is None else jnp.where(chunk_at == chunk, picked, value)
    return value


def tiles_together(rows):
    return T_ALL[min(rows, len(T_ALL)) - 1]


@functools.cache
def pair_plan(cells_x, cells_y, cells_z):
    corners = [(x, y, z) for x in (0, 1) for y in (0, 1) for z in (0, 1)]
    kinds = [
        (low, high)
        for n, low in enumerate(corners)
        for high in corners[n:]
        if all(min(i, j) == 0 for i, j in zip(low, high))
    ]
    own = [(x, y, z) for x in range(cells_x) for y in range(cells_y) for z in range(cells_z)]
    pairs = [
        tuple(tuple(i + j for i, j in zip(base, corner)) for corner in kind) for base in own for kind in kinds
    ]
    rows = {cell: [] for cell in own}
    later = []
    full = lambda cell: all(i % 2 == 0 for i in cell)
    for low, high in pairs:
        if low in rows and high in rows and low != high and full(low) != full(high):
            rows[high if full(low) else low].append(low if full(low) else high)
        elif low in rows and high not in rows:
            rows[low].append(high)
        elif high in rows and low not in rows:
            rows[high].append(low)
        elif low == high:
            rows[low].append(high)
        else:
            later.append((low, high))
    outside = [pair for pair in later if pair[0] not in rows]
    for low, high in later:
        if low in rows:
            short, other = sorted((low, high), key=lambda cell: (len(rows[cell]), cell))
            rows[short].append(other)
    while outside:
        names = sorted({cell for pair in outside for cell in pair})
        best = max(names, key=lambda cell: sum(cell in pair for pair in outside))
        rows[best] = [pair[1] if pair[0] == best else pair[0] for pair in outside if best in pair]
        outside = [pair for pair in outside if best not in pair]
    return tuple((cell, tuple(others)) for cell, others in rows.items())


def pair_terms(column, row, dist_floor):
    dx = column[0] - row[0]
    dy = column[1] - row[1]
    dz = column[2] - row[2]
    dist_sq = dx * dx + dy * dy + dz * dz
    inverse = lax.rsqrt(dist_sq)
    dist = pl.reciprocal(inverse, approx=True)
    inv_reach = jnp.minimum(inverse, 1.0 / dist_floor)
    gap = (column[3] + row[3]) - dist
    cut = jnp.maximum(SCALE * SCALE - dist_sq, 0.0)
    screened = (column[4] * row[4]) * jnp.exp2(gap) * (cut * cut)
    weight = inv_reach * (jnp.maximum(gap, 0.0) + screened * ((inv_reach + math.log(2.0)) * inv_reach))
    return weight * dx, weight * dy, weight * dz


def pair_kernel(
    sizes, coords, own, first_halo, second_halo, third_halo, packed, out, table, kept,
    sums, spread_rows, raw, pos, arms, lane_at, chunk_at, held, order, wide, row_force, column_force, contrib,
):
    cells_x, cells_y, cells_z, count_x, count_y, count_z, owned = sizes
    chunks = table.shape[1]
    unpack(packed, owned, spread_rows, table)
    ext_y, ext_z = cells_y + 1, cells_z + 1
    cells = (cells_x + 1) * ext_y * ext_z
    padded = raw.shape[0] // ROWS

    def at(x, y, z):
        return (x * ext_y + y) * ext_z + z

    def put(cell, ref, index):
        raw[cell * ROWS : (cell + 1) * ROWS, :] = ref[index * ROWS : (index + 1) * ROWS, :]

    kept[...] = own[...]
    extents = (cells_x, cells_y, cells_z)
    halos = (first_halo, second_halo, third_halo)
    for place_at in itertools.product(*[range(extent + 1) for extent in extents]):
        source, shape = own, list(extents)
        for step, axis in enumerate(HALO_ORDER):
            if place_at[axis] == extents[axis]:
                source = halos[step]
                shape = [extent + (HALO_ORDER.index(k) < step) for k, extent in enumerate(extents)]
                shape[axis] = 1
        index = 0
        for k in range(3):
            index = index * shape[k] + (0 if shape[k] == 1 else place_at[k])
        put(at(*place_at), source, index)
    for cell in range(cells, padded):
        raw[cell * ROWS : (cell + 1) * ROWS, :] = jnp.zeros((ROWS, LANES), f32)
    for cell in range(cells):
        held[cell] = jnp.max(raw[cell * ROWS + 6 : cell * ROWS + 7, :]).astype(i32)

    coord_x, coord_y, coord_z = coords[0], coords[1], coords[2]

    def place(group, carry):
        first = pl.multiple_of(group * 64, 64)
        load = lambda k: raw[pl.ds(first + k, 8, stride=ROWS), :]
        cell = group * 8 + lax.broadcasted_iota(i32, (8, LANES), 0)
        cell_x = sum((cell >= n * ext_y * ext_z).astype(i32) for n in range(1, cells_x + 1))
        rest = cell - cell_x * (ext_y * ext_z)
        cell_y = sum((rest >= n * ext_z).astype(i32) for n in range(1, cells_y + 1))
        cell_z = rest - cell_y * ext_z
        code = load(5).astype(i32)
        beyond = [
            (cell_now >= cells_now).astype(i32)
            for cell_now, cells_now in ((cell_x, cells_x), (cell_y, cells_y), (cell_z, cells_z))
        ]
        owners, lanes = owner_at(code, (coord_x, coord_y, coord_z), (count_x, count_y, count_z), beyond)
        lane_at[pl.ds(pl.multiple_of(group * 8, 8), 8), :] = lanes
        chunk_at[pl.ds(pl.multiple_of(group * 8, 8), 8), :] = owners
        pose = [lookup(lambda n, k=k: table[k, n : n + 1, :], lanes, owners, chunks) for k in range(12)]
        local = [load(k) for k in range(3)]
        cell_at = (cell_x, cell_y, cell_z)
        extents = (cells_x, cells_y, cells_z)
        for k in range(3):
            arm = pose[3 * k] * local[0] + pose[3 * k + 1] * local[1] + pose[3 * k + 2] * local[2]
            arms[k, pl.ds(pl.multiple_of(group * 8, 8), 8), :] = arm
            box = float(extents[k] * (count_x, count_y, count_z)[k])
            corner = ((coord_x, coord_y, coord_z)[k] * extents[k]).astype(f32)
            middle = cell_at[k].astype(f32) + 0.5
            inside = arm + pose[9 + k] - corner - middle
            inside = inside - box * jnp.floor(inside * (1.0 / box) + 0.5)
            pos[pl.ds(first + k, 8, stride=ROWS), :] = (inside + middle) * SCALE
        radius = load(4) * SCALE
        pos[pl.ds(first + 3, 8, stride=ROWS), :] = radius
        pos[pl.ds(first + 4, 8, stride=ROWS), :] = load(3) * CHARGE_SCALE * jnp.exp2(-radius)
        return carry

    for k in range(5, ROWS):
        for group in range(padded // 8):
            pos[pl.ds(group * 64 + k, 8, stride=ROWS), :] = jnp.zeros((8, LANES), f32)
    lax.fori_loop(0, padded // 8, place, 0)
    row_force[...] = jnp.zeros(row_force.shape, f32)
    plan = pair_plan(cells_x, cells_y, cells_z)
    listed = [at(*column) for column, _ in plan]
    listed += [listed[-1]] * (-len(listed) % SP)
    for n, cell in enumerate(listed):
        order[n] = cell
    kind = lax.broadcasted_iota(i32, (32, 5 * LANES), 1) // LANES
    part = lax.broadcasted_iota(i32, (32, 5 * LANES), 0)
    picker = jnp.where((part % 8 == kind) & (part < 24), 1.0, 0.0).astype(jnp.bfloat16)

    def spread(step, carry):
        for n in range(SP):
            cell = order[step * SP + n]
            value = pos[pl.ds(pl.multiple_of(cell * ROWS, 8), 8), :]
            high = value.astype(jnp.bfloat16).astype(f32)
            rest = value - high
            middle = rest.astype(jnp.bfloat16).astype(f32)
            low = rest - middle
            parts = jnp.concatenate([high, middle, low, jnp.zeros_like(low)], axis=0).astype(jnp.bfloat16)
            out_wide = lax.dot_general(parts, picker, (((0,), (0,)), ((), ())), preferred_element_type=f32)
            for k in range(5):
                wide[step * SP + n, k, :, :] = out_wide[:, k * LANES : (k + 1) * LANES]
        return carry

    lax.fori_loop(0, len(listed) // SP, spread, 0)

    for number, (column, rows) in enumerate(plan):
        column_cell = at(*column)
        row_cells = [at(*row) for row in rows]

        def tile_pairs(first, together, step, inner, number=number, column_cell=column_cell, row_cells=row_cells):
            spans, cols = [], []
            for n in range(together):
                span = pl.ds(pl.multiple_of((first + step * together + n) * 8, 8), 8)
                spans.append(span)
                cols.append([wide[number, k, span, :] for k in range(5)])
            sums = [[None] * 3 for _ in range(together)]
            for row_cell in row_cells:
                row = [
                    jnp.broadcast_to(pos[row_cell * ROWS + k : row_cell * ROWS + k + 1, :], (8, LANES))
                    for k in range(5)
                ]
                back = [None] * 3
                for n in range(together):
                    parts = pair_terms(cols[n], row, min_reach * SCALE)
                    for k in range(3):
                        sums[n][k] = parts[k] if sums[n][k] is None else sums[n][k] + parts[k]
                        back[k] = parts[k] if back[k] is None else back[k] + parts[k]
                if row_cell != column_cell:
                    span = slice(row_cell * ROWS, row_cell * ROWS + ROWS)
                    for k in range(3):
                        row_force[k, span, :] = row_force[k, span, :] - back[k]
            for n in range(together):
                for k in range(3):
                    column_force[number, k, spans[n], :] = sums[n][k]
            return inner

        tiles = (held[column_cell] + 7) // 8
        together = tiles_together(len(rows))
        whole = tiles // together
        lax.fori_loop(0, whole, functools.partial(tile_pairs, 0, together), 0)
        rest = tiles - whole * together
        if together >= 4:
            lax.fori_loop(0, (rest + 1) // 2, functools.partial(tile_pairs, whole * together, 2), 0)
        elif together > 1:
            lax.fori_loop(0, rest, functools.partial(tile_pairs, whole * together, 1), 0)

    ones = jnp.where(lax.broadcasted_iota(i32, (16, 2 * LANES), 0) == 0, 1.0, 0.0).astype(jnp.bfloat16)

    def fold_line(number):
        value = column_force[number].reshape(3 * LANES, LANES)
        high = value.astype(jnp.bfloat16)
        low = (value - high.astype(f32)).astype(jnp.bfloat16)
        both = jnp.concatenate([high, low], axis=1)
        return lax.dot_general(ones, both, (((1,), (1,)), ((), ())), preferred_element_type=f32)

    def fold(first, many):
        lines = [fold_line(first + n) for n in range(many)]
        for n in range(many):
            span = pl.ds(pl.multiple_of(order[first + n] * ROWS, 8), 8)
            for k in range(3):
                row_force[k, span, :] += lines[n][:8, k * LANES : (k + 1) * LANES]

    def fold_step(step, carry):
        fold(step * FO, FO)
        return carry

    even = len(plan) // FO
    lax.fori_loop(0, even, fold_step, 0)
    fold(even * FO, len(plan) - even * FO)

    def twist(group, carry):
        first = pl.multiple_of(group * 64, 64)
        span = pl.ds(pl.multiple_of(group * 8, 8), 8)
        force = []
        filled = lax.broadcasted_iota(i32, (8, LANES), 1).astype(f32) < raw[pl.ds(first + 6, 8, stride=ROWS), :]
        for k in range(3):
            total = row_force[k, pl.ds(first, 8, stride=ROWS), :]
            for n in range(1, 8):
                total = total + row_force[k, pl.ds(first + n, 8, stride=ROWS), :]
            force.append(jnp.where(filled, total * (clash_gain / SCALE), 0.0))
        arm = [arms[k, span, :] for k in range(3)]
        rows = force + [
            arm[1] * force[2] - arm[2] * force[1],
            arm[2] * force[0] - arm[0] * force[2],
            arm[0] * force[1] - arm[1] * force[0],
        ]
        for k, value in enumerate(rows):
            contrib[pl.ds(first + k, 8, stride=ROWS), :] = value
        for k in (6, 7):
            contrib[pl.ds(first + k, 8, stride=ROWS), :] = jnp.zeros((8, LANES), f32)
        return carry

    lax.fori_loop(0, padded // 8, twist, 0)

    body = lax.broadcasted_iota(i32, (LANES, LANES), 0)

    def gather_sums(step, total):
        lefts, rights = [], []
        for n in range(GA):
            cell = step * GA + n
            value = contrib[pl.ds(pl.multiple_of(cell * ROWS, 8), 8), :]
            high = value.astype(jnp.bfloat16).astype(f32)
            low = value - high
            owner = jnp.broadcast_to(chunk_at[pl.ds(cell, 1), :], (8, LANES))
            member = jnp.broadcast_to(lane_at[pl.ds(cell, 1), :], (LANES, LANES)) == body
            pieces = []
            for chunk in range(chunks):
                mine = owner == chunk
                pieces.append(jnp.where(mine, high, 0.0))
                pieces.append(jnp.where(mine, low, 0.0))
            lefts.append(jnp.concatenate(pieces, axis=0).astype(jnp.bfloat16))
            rights.append(jnp.where(member, 1.0, 0.0).astype(jnp.bfloat16))
        left = jnp.concatenate(lefts, axis=1)
        right = jnp.concatenate(rights, axis=1)
        return total + lax.dot_general(left, right, (((1,), (1,)), ((), ())), preferred_element_type=f32)

    total = lax.fori_loop(0, padded // GA, gather_sums, jnp.zeros((chunks * 16, LANES), f32))
    sums[...] = total
    for first in range(0, chunks, 8):
        many = min(8, chunks - first)
        for k in range(6):
            out[k, first : first + many, :] = (
                sums[pl.ds(first * 16 + k, many, stride=16), :] + sums[pl.ds(first * 16 + 8 + k, many, stride=16), :]
            )


def advance_rows(pose, force, torque, mobility, noise):
    centre = [pose[9 + k] + move_gain * mobility[0] * force[k] + noise[k] for k in range(3)]
    spin = [0.5 * (turn_gain * mobility[1] * torque[k] + noise[3 + k]) for k in range(3)]
    spin_sq = spin[0] * spin[0] + spin[1] * spin[1] + spin[2] * spin[2]
    factor = 2.0 / (1.0 + spin_sq)
    skew = [[None, -spin[2], spin[1]], [spin[2], None, -spin[0]], [-spin[1], spin[0], None]]
    rows = []
    for r in range(3):
        turn = []
        for c in range(3):
            inner = spin[r] * spin[c]
            turn.append(1.0 + factor * (inner - spin_sq) if r == c else factor * (skew[r][c] + inner))
        for c in range(3):
            rows.append(turn[0] * pose[c] + turn[1] * pose[3 + c] + turn[2] * pose[6 + c])
    return rows + centre


def move_kernel(sizes, coords, own, table, totals, others, stepped, positions, fresh):
    cells_x, cells_y, cells_z, count_x, count_y, count_z, owned = sizes
    chunks = table.shape[1]
    for first in range(0, chunks, 8):
        many = min(8, chunks - first)
        row = [table[k, first : first + many, :] for k in range(BODY_ROWS)]
        total = [
            totals[k, first : first + many, :] + others[k, first : first + many, :]
            for k in range(6)
        ]
        new = advance_rows(row[:12], total[:3], total[3:], row[12:14], row[14:20])
        for k in range(12):
            fresh[pl.ds(first * 16 + k, many, stride=16), :] = new[k]
    mine = ((coords[0] * count_y + coords[1]) * (count_z // 4) + (coords[2] >> 2)) * 16
    turned = pltpu.roll(
        fresh[pl.ds(pl.multiple_of(mine, 16), 16), :], (4 - (coords[2] & 3)) * SEGMENT, axis=1
    )
    stepped[...] = turned[:12, :owned]
    for first in range(0, cells_x * cells_y * cells_z, 8):
        load = lambda k: own[pl.ds(first * ROWS + k, 8, stride=ROWS), :]
        owners, lanes = owner_at(
            load(5).astype(i32), (coords[0], coords[1], coords[2]), (count_x, count_y, count_z)
        )
        pose = [
            lookup(lambda n, k=k: fresh[n * 16 + k : n * 16 + k + 1, :], lanes, owners, chunks) for k in range(12)
        ]
        local = [load(k) for k in range(3)]
        for k in range(3):
            arm = pose[3 * k] * local[0] + pose[3 * k + 1] * local[1] + pose[3 * k + 2] * local[2]
            positions[k, first : first + 8, :] = arm + pose[9 + k]


def pair_sums(sizes, coords, own, first_halo, second_halo, third_halo, packed):
    cells_x, cells_y, cells_z = sizes[:3]
    chunks = packed.shape[0] // (4 * PACKED)
    vmem = pl.BlockSpec(memory_space=pltpu.VMEM)
    smem = pl.BlockSpec(memory_space=pltpu.SMEM)
    cells = (cells_x + 1) * (cells_y + 1) * (cells_z + 1)
    padded = -(-cells // 16) * 16
    columns = -(-len(pair_plan(cells_x, cells_y, cells_z)) // SP) * SP
    return pl.pallas_call(
        functools.partial(pair_kernel, sizes),
        out_shape=(
            jax.ShapeDtypeStruct((6, chunks, LANES), f32),
            jax.ShapeDtypeStruct((BODY_ROWS, chunks, LANES), f32),
            jax.ShapeDtypeStruct(own.shape, f32),
        ),
        in_specs=[smem] + [vmem] * 5,
        out_specs=(vmem, vmem, vmem),
        scratch_shapes=[
            pltpu.VMEM((chunks * 16, LANES), f32),
            pltpu.VMEM((BODY_ROWS // PACKED,) + packed.shape, f32),
            pltpu.VMEM((padded * ROWS, LANES), f32),
            pltpu.VMEM((padded * ROWS, LANES), f32),
            pltpu.VMEM((3, padded, LANES), f32),
            pltpu.VMEM((padded, LANES), i32),
            pltpu.VMEM((padded, LANES), i32),
            pltpu.SMEM((padded,), i32),
            pltpu.SMEM((padded,), i32),
            pltpu.VMEM((columns, 5, LANES, LANES), f32),
            pltpu.VMEM((3, padded * ROWS, LANES), f32),
            pltpu.VMEM((columns, 3, LANES, LANES), f32),
            pltpu.VMEM((padded * ROWS, LANES), f32),
        ],
        compiler_params=pltpu.CompilerParams(vmem_limit_bytes=PAIR_VMEM),
    )(coords, own, first_halo, second_halo, third_halo, packed)


def from_next(block, axis):
    count = lax.axis_size(axis)
    return lax.ppermute(block, axis, [((i + 1) % count, i) for i in range(count)])


def from_partner(block, axis, mask):
    return lax.ppermute(block, axis, [(i ^ mask, i) for i in range(lax.axis_size(axis))])


def per_device(body_local, charges, radii, body_slot, cell_counts, poses, mobility, noise):
    cells_x, cells_y, cells_z, width = charges.shape
    owned = poses.shape[1]
    axes = ("gx", "gy", "gz")
    counts = tuple(lax.axis_size(axis) for axis in axes)
    devices = math.prod(counts)
    assert owned <= SEGMENT and BODY_ROWS // PACKED * owned <= LANES and width == LANES
    assert counts[2] % 4 == 0 and all(count & (count - 1) == 0 for count in counts)
    coords = jnp.stack([lax.axis_index(axis).astype(i32) for axis in axes])
    own_cells = cells_x * cells_y * cells_z
    vmem = pl.BlockSpec(memory_space=pltpu.VMEM)
    smem = pl.BlockSpec(memory_space=pltpu.SMEM)

    first_axis = HALO_ORDER[0]
    face_cells = own_cells // (cells_x, cells_y, cells_z)[first_axis]
    own, face, bodies = pl.pallas_call(
        functools.partial(prep_kernel, (cells_x, cells_y, cells_z, owned), first_axis),
        out_shape=(
            jax.ShapeDtypeStruct((own_cells * ROWS, LANES), f32),
            jax.ShapeDtypeStruct((face_cells * ROWS, LANES), f32),
            jax.ShapeDtypeStruct((devices, PACKED, LANES), f32),
        ),
        in_specs=[smem] + [vmem] * 7,
        out_specs=(vmem, vmem, vmem),
        scratch_shapes=[pltpu.VMEM((24, LANES), f32)],
    )(cell_counts, body_local, charges, radii, body_slot, poses, mobility, noise)
    packed = lax.all_to_all(bodies, axes, 0, 0).reshape(devices * PACKED, LANES)

    extended = own.reshape(cells_x, cells_y, cells_z, ROWS, LANES)
    halos = []
    for axis in HALO_ORDER:
        shape = extended.shape[:axis] + (1,) + extended.shape[axis + 1 :]
        if halos:
            face = lax.slice_in_dim(extended, 0, 1, axis=axis).reshape(-1, LANES)
        halos.append(from_next(face, axes[axis]))
        extended = jnp.concatenate([extended, halos[-1].reshape(shape)], axis=axis)

    sizes = (cells_x, cells_y, cells_z) + counts + (owned,)
    totals, table, kept = pair_sums(sizes, coords, own, *halos, packed)

    others = jnp.zeros_like(totals)
    for axis in ("gy", "gx", "gz"):
        step = 1
        while step < lax.axis_size(axis):
            totals = totals + others
            others = from_partner(totals, axis, step)
            step *= 2

    stepped, positions = pl.pallas_call(
        functools.partial(move_kernel, sizes),
        out_shape=(
            jax.ShapeDtypeStruct((12, owned), f32),
            jax.ShapeDtypeStruct((3, own_cells, LANES), f32),
        ),
        in_specs=[smem] + [vmem] * 4,
        out_specs=(vmem, vmem),
        scratch_shapes=[pltpu.VMEM((table.shape[1] * 16, LANES), f32)],
        compiler_params=pltpu.CompilerParams(vmem_limit_bytes=SMALL_VMEM),
    )(coords, kept, table, totals, others)
    return (stepped, positions.reshape(3, cells_x, cells_y, cells_z, width))


def solution(mesh):
    placed = (
        P(None, "gx", "gy", "gz", None),
        P("gx", "gy", "gz", None),
        P("gx", "gy", "gz", None),
        P("gx", "gy", "gz", None),
        P("gx", "gy", "gz"),
        P(None, ("gx", "gy", "gz")),
        P(None, ("gx", "gy", "gz")),
        P(None, ("gx", "gy", "gz")),
    )
    return jax.shard_map(
        per_device,
        mesh=mesh,
        in_specs=placed,
        out_specs=(P(None, ("gx", "gy", "gz")), P(None, "gx", "gy", "gz", None)),
        check_vma=False,
    )
```

```python
import functools
import itertools
import math

import jax
import jax.numpy as jnp
from jax import lax
from jax.experimental import pallas as pl
from jax.experimental.pallas import tpu as pltpu
from jax.sharding import PartitionSpec as P

min_reach = 0.15
clash_gain = 20.0
debye_length = 0.5
move_gain = 0.02
turn_gain = 0.01

LANES = 128
ROWS = 8
BODY_ROWS = 20
PACKED = 4
SEGMENT = 32
SCALE = 1.0 / (debye_length * math.log(2.0))
CHARGE_SCALE = math.sqrt(1.0 / (clash_gain * SCALE))
EMPTY = -20.0

f32 = jnp.float32
i32 = jnp.int32

T_ALL = (4, 4, 4, 4, 4, 4, 2, 2, 2, 2, 2, 2)
SP, FO, GA = 24, 8, 48
HALO_ORDER = (1, 0, 2)
SMALL_VMEM = 8 * 1024 * 1024
PAIR_VMEM = 24 * 1024 * 1024


def unpack(packed, owned, spread_rows, table):
    per_row = BODY_ROWS // PACKED
    row = lax.broadcasted_iota(i32, (8, LANES), 0)
    lane = lax.broadcasted_iota(i32, (8, LANES), 1)
    for first in range(0, packed.shape[0], 8):
        value = packed[first : first + 8, :]
        segment = ((first + row) // PACKED) % 4
        inside = lane - segment * SEGMENT
        valid = (inside >= 0) & (inside < owned)
        for j in range(per_row):
            index = jnp.where(valid, inside + j * owned, 0)
            picked = jnp.take_along_axis(value, index, axis=1)
            spread_rows[j, first : first + 8, :] = jnp.where(valid, picked, 0.0)
    chunks = table.shape[1]
    for m in range(BODY_ROWS):
        for first in range(0, chunks, 8):
            many = min(8, chunks - first)
            parts = [
                spread_rows[m % per_row, pl.ds((first * 4 + c) * PACKED + m // per_row, many, stride=4 * PACKED), :]
                for c in range(4)
            ]
            table[m, first : first + many, :] = (parts[0] + parts[1]) + (parts[2] + parts[3])


def owner_at(code, coords, counts, beyond=(0, 0, 0)):
    steps = ((code >> 9) - 1, ((code >> 7) & 3) - 1, ((code >> 5) & 3) - 1)
    x, y, z = [(step + coords[k] + beyond[k]) & (counts[k] - 1) for k, step in enumerate(steps)]
    chunk = (x * counts[1] + y) * (counts[2] // 4) + (z >> 2)
    return chunk, (z & 3) * SEGMENT + (code & (SEGMENT - 1))


def prep_kernel(sizes, axis, counts, local, charges, radii, slots, poses, mobility, noise, own, face, bodies, rows):
    cells_x, cells_y, cells_z, owned = sizes
    per_row = BODY_ROWS // PACKED
    rows[...] = jnp.zeros(rows.shape, f32)
    rows[0:12, :owned] = poses[...]
    rows[12:14, :owned] = mobility[...]
    rows[14:20, :owned] = noise[...]
    packed = rows[pl.ds(0, PACKED, stride=per_row), :]
    for j in range(1, per_row):
        packed = packed + pltpu.roll(rows[pl.ds(j, PACKED, stride=per_row), :], j * owned, axis=1)
    for device in range(bodies.shape[0]):
        bodies[device] = packed
    lane = lax.broadcasted_iota(i32, (cells_z, LANES), 1)
    row = lax.broadcasted_iota(i32, (cells_z, LANES), 0)
    for x in range(cells_x):
        for y in range(cells_y):
            base = (x * cells_y + y) * cells_z * ROWS
            count = jnp.zeros((cells_z, LANES), i32)
            for z in range(cells_z):
                count = jnp.where(row == z, counts[x, y, z], count)
            filled = lane < count
            slot = slots[x, y].astype(f32)
            offset = jnp.floor((slot + 0.5) * (1.0 / owned))
            body = slot - offset * owned
            step_x = jnp.floor((offset + 0.5) * (1.0 / 9.0))
            step_y = jnp.floor((offset - 9.0 * step_x + 0.5) * (1.0 / 3.0))
            step_z = offset - 9.0 * step_x - 3.0 * step_y
            code = body + 32.0 * step_z + 128.0 * step_y + 512.0 * step_x
            rows = [
                local[0, x, y],
                local[1, x, y],
                local[2, x, y],
                jnp.where(filled, charges[x, y], 0.0),
                jnp.where(filled, radii[x, y], EMPTY / SCALE),
                code,
                count.astype(f32),
                jnp.zeros((cells_z, LANES), f32),
            ]
            for k, value in enumerate(rows):
                own[pl.ds(base + k, cells_z, stride=ROWS), :] = value
    at = 0
    for x in range(1 if axis == 0 else cells_x):
        for y in range(1 if axis == 1 else cells_y):
            for z in range(1 if axis == 2 else cells_z):
                base = ((x * cells_y + y) * cells_z + z) * ROWS
                face[at : at + ROWS, :] = own[base : base + ROWS, :]
                at += ROWS


def lookup(table_row, lane_at, chunk_at, chunks):
    value = None
    for chunk in range(chunks):
        row = jnp.broadcast_to(table_row(chunk), lane_at.shape)
        picked = jnp.take_along_axis(row, lane_at, axis=1)
        value = picked if value is None else jnp.where(chunk_at == chunk, picked, value)
    return value


def tiles_together(rows):
    return T_ALL[min(rows, len(T_ALL)) - 1]


@functools.cache
def pair_plan(cells_x, cells_y, cells_z):
    corners = [(x, y, z) for x in (0, 1) for y in (0, 1) for z in (0, 1)]
    kinds = [
        (low, high)
        for n, low in enumerate(corners)
        for high in corners[n:]
        if all(min(i, j) == 0 for i, j in zip(low, high))
    ]
    own = [(x, y, z) for x in range(cells_x) for y in range(cells_y) for z in range(cells_z)]
    pairs = [
        tuple(tuple(i + j for i, j in zip(base, corner)) for corner in kind) for base in own for kind in kinds
    ]
    rows = {cell: [] for cell in own}
    later = []
    full = lambda cell: all(i % 2 == 0 for i in cell)
    for low, high in pairs:
        if low in rows and high in rows and low != high and full(low) != full(high):
            rows[high if full(low) else low].append(low if full(low) else high)
        elif low in rows and high not in rows:
            rows[low].append(high)
        elif high in rows and low not in rows:
            rows[high].append(low)
        elif low == high:
            rows[low].append(high)
        else:
            later.append((low, high))
    outside = [pair for pair in later if pair[0] not in rows]
    for low, high in later:
        if low in rows:
            short, other = sorted((low, high), key=lambda cell: (len(rows[cell]), cell))
            rows[short].append(other)
    while outside:
        names = sorted({cell for pair in outside for cell in pair})
        best = max(names, key=lambda cell: sum(cell in pair for pair in outside))
        rows[best] = [pair[1] if pair[0] == best else pair[0] for pair in outside if best in pair]
        outside = [pair for pair in outside if best not in pair]
    return tuple((cell, tuple(others)) for cell, others in rows.items())


def pair_terms(column, row, dist_floor):
    dx = column[0] - row[0]
    dy = column[1] - row[1]
    dz = column[2] - row[2]
    dist_sq = dx * dx + dy * dy + dz * dz
    inverse = lax.rsqrt(dist_sq)
    dist = pl.reciprocal(inverse, approx=True)
    inv_reach = jnp.minimum(inverse, 1.0 / dist_floor)
    gap = (column[3] + row[3]) - dist
    cut = jnp.maximum(SCALE * SCALE - dist_sq, 0.0)
    screened = (column[4] * row[4]) * jnp.exp2(gap) * (cut * cut)
    weight = inv_reach * (jnp.maximum(gap, 0.0) + screened * ((inv_reach + math.log(2.0)) * inv_reach))
    return weight * dx, weight * dy, weight * dz


def pair_kernel(
    sizes, coords, own, first_halo, second_halo, third_halo, packed, out, table, kept,
    sums, spread_rows, raw, pos, arms, lane_at, chunk_at, held, order, wide, row_force, column_force, contrib,
):
    cells_x, cells_y, cells_z, count_x, count_y, count_z, owned = sizes
    chunks = table.shape[1]
    unpack(packed, owned, spread_rows, table)
    ext_y, ext_z = cells_y + 1, cells_z + 1
    cells = (cells_x + 1) * ext_y * ext_z
    padded = raw.shape[0] // ROWS

    def at(x, y, z):
        return (x * ext_y + y) * ext_z + z

    def put(cell, ref, index):
        raw[cell * ROWS : (cell + 1) * ROWS, :] = ref[index * ROWS : (index + 1) * ROWS, :]

    kept[...] = own[...]
    extents = (cells_x, cells_y, cells_z)
    halos = (first_halo, second_halo, third_halo)
    for place_at in itertools.product(*[range(extent + 1) for extent in extents]):
        source, shape = own, list(extents)
        for step, axis in enumerate(HALO_ORDER):
            if place_at[axis] == extents[axis]:
                source = halos[step]
                shape = [extent + (HALO_ORDER.index(k) < step) for k, extent in enumerate(extents)]
                shape[axis] = 1
        index = 0
        for k in range(3):
            index = index * shape[k] + (0 if shape[k] == 1 else place_at[k])
        put(at(*place_at), source, index)
    for cell in range(cells, padded):
        raw[cell * ROWS : (cell + 1) * ROWS, :] = jnp.zeros((ROWS, LANES), f32)
    for cell in range(cells):
        held[cell] = jnp.max(raw[cell * ROWS + 6 : cell * ROWS + 7, :]).astype(i32)

    coord_x, coord_y, coord_z = coords[0], coords[1], coords[2]

    def place(group, carry):
        first = pl.multiple_of(group * 64, 64)
        load = lambda k: raw[pl.ds(first + k, 8, stride=ROWS), :]
        cell = group * 8 + lax.broadcasted_iota(i32, (8, LANES), 0)
        cell_x = sum((cell >= n * ext_y * ext_z).astype(i32) for n in range(1, cells_x + 1))
        rest = cell - cell_x * (ext_y * ext_z)
        cell_y = sum((rest >= n * ext_z).astype(i32) for n in range(1, cells_y + 1))
        cell_z = rest - cell_y * ext_z
        code = load(5).astype(i32)
        beyond = [
            (cell_now >= cells_now).astype(i32)
            for cell_now, cells_now in ((cell_x, cells_x), (cell_y, cells_y), (cell_z, cells_z))
        ]
        owners, lanes = owner_at(code, (coord_x, coord_y, coord_z), (count_x, count_y, count_z), beyond)
        lane_at[pl.ds(pl.multiple_of(group * 8, 8), 8), :] = lanes
        chunk_at[pl.ds(pl.multiple_of(group * 8, 8), 8), :] = owners
        pose = [lookup(lambda n, k=k: table[k, n : n + 1, :], lanes, owners, chunks) for k in range(12)]
        local = [load(k) for k in range(3)]
        cell_at = (cell_x, cell_y, cell_z)
        extents = (cells_x, cells_y, cells_z)
        for k in range(3):
            arm = pose[3 * k] * local[0] + pose[3 * k + 1] * local[1] + pose[3 * k + 2] * local[2]
            arms[k, pl.ds(pl.multiple_of(group * 8, 8), 8), :] = arm
            box = float(extents[k] * (count_x, count_y, count_z)[k])
            corner = ((coord_x, coord_y, coord_z)[k] * extents[k]).astype(f32)
            middle = cell_at[k].astype(f32) + 0.5
            inside = arm + pose[9 + k] - corner - middle
            inside = inside - box * jnp.floor(inside * (1.0 / box) + 0.5)
            pos[pl.ds(first + k, 8, stride=ROWS), :] = (inside + middle) * SCALE
        radius = load(4) * SCALE
        pos[pl.ds(first + 3, 8, stride=ROWS), :] = radius
        pos[pl.ds(first + 4, 8, stride=ROWS), :] = load(3) * CHARGE_SCALE * jnp.exp2(-radius)
        return carry

    for k in range(5, ROWS):
        for group in range(padded // 8):
            pos[pl.ds(group * 64 + k, 8, stride=ROWS), :] = jnp.zeros((8, LANES), f32)
    lax.fori_loop(0, padded // 8, place, 0)
    row_force[...] = jnp.zeros(row_force.shape, f32)
    plan = pair_plan(cells_x, cells_y, cells_z)
    listed = [at(*column) for column, _ in plan]
    listed += [listed[-1]] * (-len(listed) % SP)
    for n, cell in enumerate(listed):
        order[n] = cell
    kind = lax.broadcasted_iota(i32, (32, 5 * LANES), 1) // LANES
    part = lax.broadcasted_iota(i32, (32, 5 * LANES), 0)
    picker = jnp.where((part % 8 == kind) & (part < 24), 1.0, 0.0).astype(jnp.bfloat16)

    def spread(step, carry):
        for n in range(SP):
            cell = order[step * SP + n]
            value = pos[pl.ds(pl.multiple_of(cell * ROWS, 8), 8), :]
            high = value.astype(jnp.bfloat16).astype(f32)
            rest = value - high
            middle = rest.astype(jnp.bfloat16).astype(f32)
            low = rest - middle
            parts = jnp.concatenate([high, middle, low, jnp.zeros_like(low)], axis=0).astype(jnp.bfloat16)
            out_wide = lax.dot_general(parts, picker, (((0,), (0,)), ((), ())), preferred_element_type=f32)
            for k in range(5):
                wide[step * SP + n, k, :, :] = out_wide[:, k * LANES : (k + 1) * LANES]
        return carry

    lax.fori_loop(0, len(listed) // SP, spread, 0)

    for number, (column, rows) in enumerate(plan):
        column_cell = at(*column)
        row_cells = [at(*row) for row in rows]

        def tile_pairs(first, together, step, inner, number=number, column_cell=column_cell, row_cells=row_cells):
            spans, cols = [], []
            for n in range(together):
                span = pl.ds(pl.multiple_of((first + step * together + n) * 8, 8), 8)
                spans.append(span)
                cols.append([wide[number, k, span, :] for k in range(5)])
            sums = [[None] * 3 for _ in range(together)]
            for row_cell in row_cells:
                row = [
                    jnp.broadcast_to(pos[row_cell * ROWS + k : row_cell * ROWS + k + 1, :], (8, LANES))
                    for k in range(5)
                ]
                back = [None] * 3
                for n in range(together):
                    parts = pair_terms(cols[n], row, min_reach * SCALE)
                    for k in range(3):
                        sums[n][k] = parts[k] if sums[n][k] is None else sums[n][k] + parts[k]
                        back[k] = parts[k] if back[k] is None else back[k] + parts[k]
                if row_cell != column_cell:
                    span = slice(row_cell * ROWS, row_cell * ROWS + ROWS)
                    for k in range(3):
                        row_force[k, span, :] = row_force[k, span, :] - back[k]
            for n in range(together):
                for k in range(3):
                    column_force[number, k, spans[n], :] = sums[n][k]
            return inner

        tiles = (held[column_cell] + 7) // 8
        together = tiles_together(len(rows))
        whole = tiles // together
        lax.fori_loop(0, whole, functools.partial(tile_pairs, 0, together), 0)
        rest = tiles - whole * together
        if together >= 4:
            lax.fori_loop(0, (rest + 1) // 2, functools.partial(tile_pairs, whole * together, 2), 0)
        elif together > 1:
            lax.fori_loop(0, rest, functools.partial(tile_pairs, whole * together, 1), 0)

    ones = jnp.where(lax.broadcasted_iota(i32, (16, 2 * LANES), 0) == 0, 1.0, 0.0).astype(jnp.bfloat16)

    def fold_line(number):
        value = column_force[number].reshape(3 * LANES, LANES)
        high = value.astype(jnp.bfloat16)
        low = (value - high.astype(f32)).astype(jnp.bfloat16)
        both = jnp.concatenate([high, low], axis=1)
        return lax.dot_general(ones, both, (((1,), (1,)), ((), ())), preferred_element_type=f32)

    def fold(first, many):
        lines = [fold_line(first + n) for n in range(many)]
        for n in range(many):
            span = pl.ds(pl.multiple_of(order[first + n] * ROWS, 8), 8)
            for k in range(3):
                row_force[k, span, :] += lines[n][:8, k * LANES : (k + 1) * LANES]

    def fold_step(step, carry):
        fold(step * FO, FO)
        return carry

    even = len(plan) // FO
    lax.fori_loop(0, even, fold_step, 0)
    fold(even * FO, len(plan) - even * FO)

    def twist(group, carry):
        first = pl.multiple_of(group * 64, 64)
        span = pl.ds(pl.multiple_of(group * 8, 8), 8)
        force = []
        filled = lax.broadcasted_iota(i32, (8, LANES), 1).astype(f32) < raw[pl.ds(first + 6, 8, stride=ROWS), :]
        for k in range(3):
            total = row_force[k, pl.ds(first, 8, stride=ROWS), :]
            for n in range(1, 8):
                total = total + row_force[k, pl.ds(first + n, 8, stride=ROWS), :]
            force.append(jnp.where(filled, total * (clash_gain / SCALE), 0.0))
        arm = [arms[k, span, :] for k in range(3)]
        rows = force + [
            arm[1] * force[2] - arm[2] * force[1],
            arm[2] * force[0] - arm[0] * force[2],
            arm[0] * force[1] - arm[1] * force[0],
        ]
        for k, value in enumerate(rows):
            contrib[pl.ds(first + k, 8, stride=ROWS), :] = value
        for k in (6, 7):
            contrib[pl.ds(first + k, 8, stride=ROWS), :] = jnp.zeros((8, LANES), f32)
        return carry

    lax.fori_loop(0, padded // 8, twist, 0)

    body = lax.broadcasted_iota(i32, (LANES, LANES), 0)

    def gather_sums(step, total):
        lefts, rights = [], []
        for n in range(GA):
            cell = step * GA + n
            value = contrib[pl.ds(pl.multiple_of(cell * ROWS, 8), 8), :]
            high = value.astype(jnp.bfloat16).astype(f32)
            low = value - high
            owner = jnp.broadcast_to(chunk_at[pl.ds(cell, 1), :], (8, LANES))
            member = jnp.broadcast_to(lane_at[pl.ds(cell, 1), :], (LANES, LANES)) == body
            pieces = []
            for chunk in range(chunks):
                mine = owner == chunk
                pieces.append(jnp.where(mine, high, 0.0))
                pieces.append(jnp.where(mine, low, 0.0))
            lefts.append(jnp.concatenate(pieces, axis=0).astype(jnp.bfloat16))
            rights.append(jnp.where(member, 1.0, 0.0).astype(jnp.bfloat16))
        left = jnp.concatenate(lefts, axis=1)
        right = jnp.concatenate(rights, axis=1)
        return total + lax.dot_general(left, right, (((1,), (1,)), ((), ())), preferred_element_type=f32)

    total = lax.fori_loop(0, padded // GA, gather_sums, jnp.zeros((chunks * 16, LANES), f32))
    sums[...] = total
    for first in range(0, chunks, 8):
        many = min(8, chunks - first)
        for k in range(6):
            out[k, first : first + many, :] = (
                sums[pl.ds(first * 16 + k, many, stride=16), :] + sums[pl.ds(first * 16 + 8 + k, many, stride=16), :]
            )


def advance_rows(pose, force, torque, mobility, noise):
    centre = [pose[9 + k] + move_gain * mobility[0] * force[k] + noise[k] for k in range(3)]
    spin = [0.5 * (turn_gain * mobility[1] * torque[k] + noise[3 + k]) for k in range(3)]
    spin_sq = spin[0] * spin[0] + spin[1] * spin[1] + spin[2] * spin[2]
    factor = 2.0 / (1.0 + spin_sq)
    skew = [[None, -spin[2], spin[1]], [spin[2], None, -spin[0]], [-spin[1], spin[0], None]]
    rows = []
    for r in range(3):
        turn = []
        for c in range(3):
            inner = spin[r] * spin[c]
            turn.append(1.0 + factor * (inner - spin_sq) if r == c else factor * (skew[r][c] + inner))
        for c in range(3):
            rows.append(turn[0] * pose[c] + turn[1] * pose[3 + c] + turn[2] * pose[6 + c])
    return rows + centre


def move_kernel(sizes, coords, own, table, totals, others, stepped, positions, fresh):
    cells_x, cells_y, cells_z, count_x, count_y, count_z, owned = sizes
    chunks = table.shape[1]
    for first in range(0, chunks, 8):
        many = min(8, chunks - first)
        row = [table[k, first : first + many, :] for k in range(BODY_ROWS)]
        total = [
            totals[k, first : first + many, :] + others[k, first : first + many, :]
            for k in range(6)
        ]
        new = advance_rows(row[:12], total[:3], total[3:], row[12:14], row[14:20])
        for k in range(12):
            fresh[pl.ds(first * 16 + k, many, stride=16), :] = new[k]
    mine = ((coords[0] * count_y + coords[1]) * (count_z // 4) + (coords[2] >> 2)) * 16
    turned = pltpu.roll(
        fresh[pl.ds(pl.multiple_of(mine, 16), 16), :], (4 - (coords[2] & 3)) * SEGMENT, axis=1
    )
    stepped[...] = turned[:12, :owned]
    for first in range(0, cells_x * cells_y * cells_z, 8):
        load = lambda k: own[pl.ds(first * ROWS + k, 8, stride=ROWS), :]
        owners, lanes = owner_at(
            load(5).astype(i32), (coords[0], coords[1], coords[2]), (count_x, count_y, count_z)
        )
        pose = [
            lookup(lambda n, k=k: fresh[n * 16 + k : n * 16 + k + 1, :], lanes, owners, chunks) for k in range(12)
        ]
        local = [load(k) for k in range(3)]
        for k in range(3):
            arm = pose[3 * k] * local[0] + pose[3 * k + 1] * local[1] + pose[3 * k + 2] * local[2]
            positions[k, first : first + 8, :] = arm + pose[9 + k]


def pair_sums(sizes, coords, own, first_halo, second_halo, third_halo, packed):
    cells_x, cells_y, cells_z = sizes[:3]
    chunks = packed.shape[0] // (4 * PACKED)
    vmem = pl.BlockSpec(memory_space=pltpu.VMEM)
    smem = pl.BlockSpec(memory_space=pltpu.SMEM)
    cells = (cells_x + 1) * (cells_y + 1) * (cells_z + 1)
    padded = -(-cells // 16) * 16
    columns = -(-len(pair_plan(cells_x, cells_y, cells_z)) // SP) * SP
    return pl.pallas_call(
        functools.partial(pair_kernel, sizes),
        out_shape=(
            jax.ShapeDtypeStruct((6, chunks, LANES), f32),
            jax.ShapeDtypeStruct((BODY_ROWS, chunks, LANES), f32),
            jax.ShapeDtypeStruct(own.shape, f32),
        ),
        in_specs=[smem] + [vmem] * 5,
        out_specs=(vmem, vmem, vmem),
        scratch_shapes=[
            pltpu.VMEM((chunks * 16, LANES), f32),
            pltpu.VMEM((BODY_ROWS // PACKED,) + packed.shape, f32),
            pltpu.VMEM((padded * ROWS, LANES), f32),
            pltpu.VMEM((padded * ROWS, LANES), f32),
            pltpu.VMEM((3, padded, LANES), f32),
            pltpu.VMEM((padded, LANES), i32),
            pltpu.VMEM((padded, LANES), i32),
            pltpu.SMEM((padded,), i32),
            pltpu.SMEM((padded,), i32),
            pltpu.VMEM((columns, 5, LANES, LANES), f32),
            pltpu.VMEM((3, padded * ROWS, LANES), f32),
            pltpu.VMEM((columns, 3, LANES, LANES), f32),
            pltpu.VMEM((padded * ROWS, LANES), f32),
        ],
        compiler_params=pltpu.CompilerParams(vmem_limit_bytes=PAIR_VMEM),
    )(coords, own, first_halo, second_halo, third_halo, packed)


def from_next(block, axis):
    count = lax.axis_size(axis)
    return lax.ppermute(block, axis, [((i + 1) % count, i) for i in range(count)])


def from_partner(block, axis, mask):
    return lax.ppermute(block, axis, [(i ^ mask, i) for i in range(lax.axis_size(axis))])


def per_device(body_local, charges, radii, body_slot, cell_counts, poses, mobility, noise):
    cells_x, cells_y, cells_z, width = charges.shape
    owned = poses.shape[1]
    axes = ("gx", "gy", "gz")
    counts = tuple(lax.axis_size(axis) for axis in axes)
    devices = math.prod(counts)
    assert owned <= SEGMENT and BODY_ROWS // PACKED * owned <= LANES and width == LANES
    assert counts[2] % 4 == 0 and all(count & (count - 1) == 0 for count in counts)
    coords = jnp.stack([lax.axis_index(axis).astype(i32) for axis in axes])
    own_cells = cells_x * cells_y * cells_z
    vmem = pl.BlockSpec(memory_space=pltpu.VMEM)
    smem = pl.BlockSpec(memory_space=pltpu.SMEM)

    first_axis = HALO_ORDER[0]
    face_cells = own_cells // (cells_x, cells_y, cells_z)[first_axis]
    own, face, bodies = pl.pallas_call(
        functools.partial(prep_kernel, (cells_x, cells_y, cells_z, owned), first_axis),
        out_shape=(
            jax.ShapeDtypeStruct((own_cells * ROWS, LANES), f32),
            jax.ShapeDtypeStruct((face_cells * ROWS, LANES), f32),
            jax.ShapeDtypeStruct((devices, PACKED, LANES), f32),
        ),
        in_specs=[smem] + [vmem] * 7,
        out_specs=(vmem, vmem, vmem),
        scratch_shapes=[pltpu.VMEM((24, LANES), f32)],
    )(cell_counts, body_local, charges, radii, body_slot, poses, mobility, noise)
    packed = lax.all_to_all(bodies, axes, 0, 0).reshape(devices * PACKED, LANES)

    extended = own.reshape(cells_x, cells_y, cells_z, ROWS, LANES)
    halos = []
    for axis in HALO_ORDER:
        shape = extended.shape[:axis] + (1,) + extended.shape[axis + 1 :]
        if halos:
            face = lax.slice_in_dim(extended, 0, 1, axis=axis).reshape(-1, LANES)
        halos.append(from_next(face, axes[axis]))
        extended = jnp.concatenate([extended, halos[-1].reshape(shape)], axis=axis)

    sizes = (cells_x, cells_y, cells_z) + counts + (owned,)
    totals, table, kept = pair_sums(sizes, coords, own, *halos, packed)

    others = jnp.zeros_like(totals)
    for axis in ("gz", "gy", "gx"):
        step = 1
        while step < lax.axis_size(axis):
            totals = totals + others
            others = from_partner(totals, axis, step)
            step *= 2

    stepped, positions = pl.pallas_call(
        functools.partial(move_kernel, sizes),
        out_shape=(
            jax.ShapeDtypeStruct((12, owned), f32),
            jax.ShapeDtypeStruct((3, own_cells, LANES), f32),
        ),
        in_specs=[smem] + [vmem] * 4,
        out_specs=(vmem, vmem),
        scratch_shapes=[pltpu.VMEM((table.shape[1] * 16, LANES), f32)],
        compiler_params=pltpu.CompilerParams(vmem_limit_bytes=SMALL_VMEM),
    )(coords, kept, table, totals, others)
    return (stepped, positions.reshape(3, cells_x, cells_y, cells_z, width))


def solution(mesh):
    placed = (
        P(None, "gx", "gy", "gz", None),
        P("gx", "gy", "gz", None),
        P("gx", "gy", "gz", None),
        P("gx", "gy", "gz", None),
        P("gx", "gy", "gz"),
        P(None, ("gx", "gy", "gz")),
        P(None, ("gx", "gy", "gz")),
        P(None, ("gx", "gy", "gz")),
    )
    return jax.shard_map(
        per_device,
        mesh=mesh,
        in_specs=placed,
        out_specs=(P(None, ("gx", "gy", "gz")), P(None, "gx", "gy", "gz", None)),
        check_vma=False,
    )
```
